32 devices in a mesh: dp: 2 (over y), ctx: 16 (over z, x, core).
Axes of the slice: x: 2, y: 2, z: 4, core: 2. Of those that a mesh axis runs over, the one named last changes fastest.
Arguments:
- positions: int32 [2, 768], P('dp', 'ctx'), may hold values from -1 to 2047, as said below
- queries: bfloat16 [2, 768, 3072], P('dp', 'ctx'), may hold values from -6 to 6
- keys: bfloat16 [2, 768, 512], P('dp', 'ctx'), may hold values from -6 to 6
- values: bfloat16 [2, 768, 512], P('dp', 'ctx'), may hold values from -6 to 6
- router_logits: float32 [2, 768], P('dp', 'ctx'), may hold values from -6 to 6
- out_cotangent: bfloat16 [2, 768, 3072], P('dp', 'ctx'), may hold values from -24 to 24
- query_gain: float32 [128], replicated, may hold values from 0.8 to 5.5
- key_gain: float32 [128], replicated, may hold values from 0.8 to 5.5
Outputs:
- block_out: bfloat16 [2, 768, 3072], P('dp', 'ctx')
- grad_queries: bfloat16 [2, 768, 3072], P('dp', 'ctx')
- grad_keys: bfloat16 [2, 768, 512], P('dp', 'ctx')
- grad_values: bfloat16 [2, 768, 512], P('dp', 'ctx')
- grad_logits: float32 [2, 768], P('dp', 'ctx')
- grad_query_gain: float32 [128], replicated
- grad_key_gain: float32 [128], replicated
The draws below stay inside these ranges and needn't reach their ends.
Inputs may be any that keep to these rules, and one draw needn't show every extreme that they name: For each sequence and each device along ctx, the device's 48 slots hold, in rising order, the positions of the device's selected tokens, all within the device's own block of 128 positions, followed by -1 in the slots it leaves unused. Every aligned run of 4 devices selects exactly 64 tokens; a device selects at most 48 tokens, and in every sequence some device selects exactly 48. The last device of every sequence selects position 2047.
All inputs are finite; a program needn't handle non-finite values.
Results may differ from the reference program's by a relative error of at most 0.023.
The reference program's roundings to bfloat16 on the way count: a program that leaves them out, or rounds other values in their place, can miss the bound.
Values may be sent and summed in bfloat16 or wider, within the bound.
A program may use at most 64 MiB of HBM per device.

```python
import math
import jax
import jax.numpy as jnp
from jax import lax

HD = 128
HQ = 24
HK = 4
TOK_DEV = 128
SEG_DEV = 4
SEL_DEV = 16
CAP = 48
SELECTED = 256
ROWS = 768
SEQS = 2
N_CTX = 16


def key_base(key):
    shape = (SEQS, ROWS, HK * HD)
    normal_part = jax.random.normal(key, shape, jnp.float32)
    return normal_part


def draw_keys(key, part):
    normal_part = key_base(key)
    return jnp.clip(normal_part, -6.0, 6.0).astype(jnp.bfloat16)


def draw_queries(key, part):
    key = jax.random.fold_in(key, 5)
    key_own = jax.random.fold_in(key, 0)
    shape = (SEQS, ROWS, HQ, HD)
    own_part = jax.random.normal(key_own, shape, jnp.float32)
    return jnp.clip(own_part, -6.0, 6.0).reshape(SEQS, ROWS, HQ * HD).astype(jnp.bfloat16)


def draw_query_gain(key, part):
    key = jax.random.fold_in(key, 7)
    return jnp.exp(jax.random.uniform(key, (HD,), jnp.float32, math.log(0.8), math.log(2.0)))


def draw_key_gain(key, part):
    key = jax.random.fold_in(key, 9)
    return jnp.exp(jax.random.uniform(key, (HD,), jnp.float32, math.log(0.8), math.log(2.0)))


def draw_out_cotangent(key, part):
    key = jax.random.fold_in(key, 13)
    key_rows = jax.random.fold_in(key, 0)
    shape = (SEQS, ROWS, HQ * HD)
    along = (jnp.arange(ROWS) // CAP).astype(jnp.float32) / (N_CTX - 1)
    rising = 1.0 + 2.0 * along
    normal_part = jnp.clip(jax.random.normal(key_rows, shape, jnp.float32), -6.0, 6.0)
    return (normal_part * rising[None, :, None]).astype(jnp.bfloat16)


def draw_positions(key, part):
    key = jax.random.fold_in(key, 17)
    key_heavy_at, key_heavy, key_full, key_cuts, key_perm = jax.random.split(key, 5)
    segments = N_CTX // SEG_DEV
    heavy_at = jax.random.randint(key_heavy_at, (SEQS, segments), 0, SEG_DEV)
    heavy_at = jnp.where(jnp.arange(segments)[None, :] == segments - 1, SEG_DEV - 1, heavy_at)
    heavy = jax.random.randint(key_heavy, (SEQS, segments), 2 * SEL_DEV, CAP + 1)
    full_segment = jax.random.randint(key_full, (SEQS, 1), 0, segments)
    heavy = jnp.where(jnp.arange(segments)[None, :] == full_segment, CAP, heavy)
    remaining = SEG_DEV * SEL_DEV - heavy
    cut_points = jax.random.randint(key_cuts, (SEQS, segments, SEG_DEV - 2), 0, remaining[..., None] + 1)
    cut_points = jnp.sort(cut_points, axis=-1)
    bounded = jnp.concatenate([jnp.zeros((SEQS, segments, 1), jnp.int32), cut_points, remaining[..., None]], axis=-1)
    others = bounded[..., 1:] - bounded[..., :-1]
    spot = jnp.arange(SEG_DEV)[None, None, :]
    other_index = jnp.clip(spot - (spot > heavy_at[..., None]).astype(jnp.int32), 0, SEG_DEV - 2)
    taken = jnp.take_along_axis(others, other_index, axis=-1)
    counts = jnp.where(spot == heavy_at[..., None], heavy[..., None], taken).reshape(SEQS, N_CTX)
    perm_keys = jax.random.split(key_perm, SEQS * N_CTX)
    shuffled = jax.vmap(lambda single: jax.random.permutation(single, TOK_DEV))(perm_keys)
    shuffled = shuffled.reshape(SEQS, N_CTX, TOK_DEV)
    rotated = (shuffled - shuffled[..., :1] + TOK_DEV - 1) % TOK_DEV
    is_last = (jnp.arange(N_CTX) == N_CTX - 1)[None, :, None]
    shuffled = jnp.where(is_last, rotated, shuffled)
    chosen = shuffled[..., :CAP]
    in_use = jnp.arange(CAP)[None, None, :] < counts[..., None]
    local_pos = jnp.sort(jnp.where(in_use, chosen, TOK_DEV), axis=-1)
    device_base = jnp.arange(N_CTX)[None, :, None] * TOK_DEV
    global_pos = jnp.where(local_pos < TOK_DEV, local_pos + device_base, -1)
    return global_pos.reshape(SEQS, N_CTX * CAP).astype(jnp.int32)


def steps_of(rng, extent, cuts, smallest, top_value):
    factor_of = 1.0
    for axis_at, shards_of in cuts:
        steps = jax.random.uniform(jax.random.fold_in(jax.random.fold_in(rng, 6), axis_at), (shards_of,), jnp.float32, smallest / len(cuts), top_value / len(cuts))
        factor_of = factor_of * jnp.repeat(jnp.exp(steps), extent[axis_at] // shards_of).reshape((-1,) + (1,) * (len(extent) - 1 - axis_at))
    return factor_of


def scatter_about(key, dims, deviation, most, pieces=(), dtype=jnp.bfloat16):
    drawn = jax.random.normal(key, dims, jnp.float32) * deviation
    if len(pieces) > 0:
        drawn = steps_of(key, dims, pieces, -0.22, 0.18) * drawn
    return jnp.clip(drawn, min=-most, max=most).astype(dtype)


def setup_inputs(seed: int = 0) -> dict:
    splits = jax.random.split(jax.random.key(seed), 9)
    positions = draw_positions(jax.random.fold_in(splits[8], 71), 0)
    queries = draw_queries(jax.random.fold_in(splits[8], 71), 0)
    keys = draw_keys(jax.random.fold_in(splits[8], 71), 0)
    values = scatter_about(splits[3], (SEQS, ROWS, HK * HD), 1.0, 6.0, ((0, 2), (1, 16)))
    router_logits = scatter_about(splits[4], (SEQS, ROWS), 2.0, 6.0, ((0, 2), (1, 16)), jnp.float32)
    out_cotangent = draw_out_cotangent(jax.random.fold_in(splits[8], 71), 0)
    query_gain = draw_query_gain(jax.random.fold_in(splits[8], 71), 0)
    key_gain = draw_key_gain(jax.random.fold_in(splits[8], 71), 0)
    return dict(positions=positions, queries=queries, keys=keys, values=values, router_logits=router_logits, out_cotangent=out_cotangent, query_gain=query_gain, key_gain=key_gain)


rope_base = 1000000.0
norm_eps = 1e-06

def rope_tables(token_pos, head_size):
    index_row = jnp.arange(head_size // 2).astype(jnp.float32)
    frequency = jnp.exp(index_row * (-2.0 * math.log(rope_base) / head_size))
    angles = token_pos.astype(jnp.float32)[:, None] * frequency[None, :]
    return (jnp.cos(angles)[:, None, :], jnp.sin(angles)[:, None, :])

def rotate(source, cos_table, sine_table, direction):
    half_size = source.shape[-1] // 2
    lead_half = source[..., :half_size]
    tail_half = source[..., half_size:]
    return jnp.concatenate([lead_half * cos_table - direction * tail_half * sine_table, direction * lead_half * sine_table + tail_half * cos_table], axis=-1)

def normalize(source, gain_vec, cos_table, sine_table, head_total):
    heads_view = source.astype(jnp.float32).reshape(source.shape[0], head_total, -1)
    inv_rms = lax.rsqrt(lax.optimization_barrier(jnp.mean(heads_view * heads_view, axis=-1, keepdims=True)) + norm_eps)
    unit_rows = heads_view * inv_rms
    return (rotate(unit_rows * gain_vec, cos_table, sine_table, 1.0), unit_rows, inv_rms)

def norm_grad(grad_rot, unit_rows, inv_rms, gain_vec, cos_table, sine_table):
    unrotated = rotate(grad_rot.astype(jnp.float32), cos_table, sine_table, -1.0)
    gain_term = lax.optimization_barrier(jnp.sum(unrotated * unit_rows, axis=(0, 1)))
    scaled = unrotated * gain_vec
    grad_input = inv_rms * (scaled - unit_rows * lax.optimization_barrier(jnp.mean(scaled * unit_rows, axis=-1, keepdims=True)))
    return (grad_input, gain_term)

def one_sequence(token_pos, queries, keys, values, router_logits, out_cotangent, query_gain, key_gain):
    is_valid = (token_pos >= 0).astype(jnp.int32)
    ordering = jnp.argsort(1 - is_valid, stable=True)[:SELECTED].astype(jnp.int32)
    chosen_pos = token_pos[ordering]
    cos_table, sine_table = rope_tables(chosen_pos, HD)
    q_rot, q_unit, q_inv = normalize(queries[ordering], query_gain, cos_table, sine_table, HQ)
    k_rot, k_unit, k_inv = normalize(keys[ordering], key_gain, cos_table, sine_table, HK)
    gating = jax.nn.sigmoid(router_logits[ordering])
    d_rows = (gating[:, None] * out_cotangent[ordering].astype(jnp.float32)).astype(jnp.bfloat16)
    q_round = q_rot.astype(jnp.bfloat16)
    k_round = k_rot.astype(jnp.bfloat16)
    q_round, k_round, d_rows = lax.optimization_barrier((q_round, k_round, d_rows))
    group_size = HQ // HK
    score_scale = 1.0 / math.sqrt(HD)
    causal = jnp.arange(SELECTED)[None, :] <= jnp.arange(SELECTED)[:, None]
    query_heads = q_round.astype(jnp.float32).reshape(SELECTED, HK, group_size, HD).transpose(1, 0, 2, 3)
    cotan_heads = d_rows.astype(jnp.float32).reshape(SELECTED, HK, group_size, HD).transpose(1, 0, 2, 3)
    key_heads = k_round.astype(jnp.float32).transpose(1, 0, 2)
    value_heads = values[ordering].astype(jnp.float32).reshape(SELECTED, HK, HD).transpose(1, 0, 2)

    def per_head(operands):
        query_part, cotan_part, key_part, value_part = operands
        scores = jnp.einsum('aqd,bd->qab', query_part, key_part) * score_scale
        scores = jnp.where(causal[None], scores, -jnp.inf)
        row_max = lax.optimization_barrier(jnp.max(scores, axis=-1, keepdims=True))
        exp_scores = jnp.exp(scores - row_max)
        probs = exp_scores / lax.optimization_barrier(jnp.sum(exp_scores, axis=-1, keepdims=True))
        prob_round = lax.optimization_barrier(probs.astype(jnp.bfloat16)).astype(jnp.float32)
        attended = lax.optimization_barrier(jnp.einsum('qab,bd->aqd', prob_round, value_part).astype(jnp.bfloat16))
        row_delta = jnp.einsum('aqd,aqd->qa', cotan_part, attended.astype(jnp.float32))
        grad_prob = jnp.einsum('aqd,bd->qab', cotan_part, value_part)
        dscore = (probs * (grad_prob - row_delta[:, :, None])).astype(jnp.bfloat16)
        dscore = lax.optimization_barrier(dscore).astype(jnp.float32)
        grad_query = (jnp.einsum('qab,bd->aqd', dscore, key_part) * score_scale).astype(jnp.bfloat16)
        grad_key = (jnp.einsum('qab,aqd->bd', dscore, query_part) * score_scale).astype(jnp.bfloat16)
        grad_value = jnp.einsum('qab,aqd->bd', prob_round, cotan_part).astype(jnp.bfloat16)
        return (attended, grad_query, grad_key, grad_value)
    attended, grad_query, grad_key, grad_value = lax.map(per_head, (query_heads, cotan_heads, key_heads, value_heads))
    attended, grad_query, grad_key = lax.optimization_barrier((attended, grad_query, grad_key))
    attended = attended.transpose(1, 0, 2, 3).reshape(SELECTED, HQ * HD)
    grad_query = grad_query.transpose(1, 0, 2, 3).reshape(SELECTED, HQ, HD)
    grad_key = grad_key.transpose(1, 0, 2).reshape(SELECTED, HK, HD)
    grad_value = grad_value.transpose(1, 0, 2).reshape(SELECTED, HK * HD)
    attended_f = attended.astype(jnp.float32)
    block_rows = (gating[:, None] * attended_f).astype(jnp.bfloat16)
    logit_rows = (1.0 - gating) * lax.optimization_barrier(jnp.sum(d_rows.astype(jnp.float32) * attended_f, axis=-1))
    query_rows, query_term = norm_grad(grad_query, q_unit, q_inv, query_gain, cos_table, sine_table)
    key_rows, key_term = norm_grad(grad_key, k_unit, k_inv, key_gain, cos_table, sine_table)
    slot_total = token_pos.shape[0]
    block_out = jnp.zeros((slot_total, HQ * HD), jnp.bfloat16).at[ordering].set(block_rows)
    grad_queries = jnp.zeros((slot_total, HQ * HD), jnp.bfloat16).at[ordering].set(query_rows.reshape(SELECTED, HQ * HD).astype(jnp.bfloat16))
    grad_keys = jnp.zeros((slot_total, HK * HD), jnp.bfloat16).at[ordering].set(key_rows.reshape(SELECTED, HK * HD).astype(jnp.bfloat16))
    grad_values = jnp.zeros((slot_total, HK * HD), jnp.bfloat16).at[ordering].set(grad_value)
    grad_logits = jnp.zeros((slot_total,), jnp.float32).at[ordering].set(logit_rows)
    return (block_out, grad_queries, grad_keys, grad_values, grad_logits, query_term, key_term)

def reference(positions, queries, keys, values, router_logits, out_cotangent, query_gain, key_gain):
    results = [one_sequence(positions[sequence], queries[sequence], keys[sequence], values[sequence], router_logits[sequence], out_cotangent[sequence], query_gain, key_gain) for sequence in range(SEQS)]
    stacked = [jnp.stack([result[member] for result in results]) for member in range(5)]
    query_total = lax.optimization_barrier(jnp.sum(jnp.stack([result[5] for result in results]), axis=0))
    key_total = lax.optimization_barrier(jnp.sum(jnp.stack([result[6] for result in results]), axis=0))
    query_total = query_total / math.sqrt(SEQS * SELECTED * HQ)
    key_total = key_total / math.sqrt(SEQS * SELECTED * HK)
    return (stacked[0], stacked[1], stacked[2], stacked[3], stacked[4], query_total, key_total)
```

```python
import functools
import math

import jax
import jax.numpy as jnp
from jax import lax
from jax.experimental import pallas as pl
from jax.experimental.pallas import tpu as pltpu
from jax.sharding import PartitionSpec as P

SEL_DEV = 16
SEG_DEV = 4

rope_base = 1000000.0
norm_eps = 1e-06

F32 = jnp.float32
BF16 = jnp.bfloat16


def dot(a, b, dims):
    return lax.dot_general(a, b, (dims, ((), ())), preferred_element_type=F32)


NN = ((1,), (0,))
NT = ((1,), (1,))
TN = ((0,), (0,))


def kernel(
    n_seg,
    n_dp,
    aux_ref,
    q_ref,
    k_ref,
    v_ref,
    c_ref,
    gain_ref,
    out_ref,
    gq_ref,
    gk_ref,
    gv_ref,
    gl_ref,
    gains_ref,
    skv,
    rkv,
    sqd,
    rqd,
    qunit,
    qinv,
    dround,
    kunit,
    kinv,
    kv_all,
    dkv_p,
    dkv_r,
    sback,
    rback,
    skb,
    rkb,
    gplane,
    gseg,
    gdp,
    kv_s,
    kv_r,
    qd_s,
    qd_r,
    z_s,
    z_r,
    dz_s,
    dz_r,
    b_s,
    b_r,
    kb_s,
    kb_r,
    g_s,
    g_r,
):
    cap, width_q = q_ref.shape
    width_k = k_ref.shape[1]
    head = gain_ref.shape[1]
    heads_k = width_k // head
    group = width_q // width_k
    gw = group * head
    sel = SEL_DEV * SEG_DEV
    pad = rkv.shape[1]
    scale = 1.0 / math.sqrt(head)

    my_dp = lax.axis_index("dp")
    my_ctx = lax.axis_index("ctx")
    seg = my_ctx // SEG_DEV
    g = my_ctx % SEG_DEV
    mate = {0: g, 1: g + 1 - 2 * (g % 2), 2: (g + 2) % 4, 3: 3 - g}
    plane = {o: seg * SEG_DEV + mate[o] for o in (1, 2, 3)}
    far = {o: (seg + o) % n_seg for o in range(1, n_seg)}
    far_dev = {o: far[o] * SEG_DEV + g for o in far}
    rows_dp = {o: (my_dp + o) % n_dp for o in range(1, n_dp)}
    order = (2, 3, 1)

    def remote(src, dst, ssem, rsem, ctx=None, dp=None):
        return pltpu.make_async_remote_copy(
            src_ref=src,
            dst_ref=dst,
            send_sem=ssem,
            recv_sem=rsem,
            device_id=(my_dp if dp is None else dp, my_ctx if ctx is None else ctx),
            device_id_type=pl.DeviceIdType.MESH,
        )

    barrier = pltpu.get_barrier_semaphore()
    peers = [(my_dp, plane[o]) for o in order]
    peers += [(my_dp, far_dev[o]) for o in far]
    peers += [(rows_dp[o], my_ctx) for o in rows_dp]
    for peer in peers:
        pl.semaphore_signal(barrier, inc=1, device_id=peer, device_id_type=pl.DeviceIdType.MESH)

    cos = aux_ref[0]
    sin = aux_ref[1]
    gate = aux_ref[2]
    valid = aux_ref[3]
    gain_q = gain_ref[0:1]
    gain_k = gain_ref[1:2]

    def normed(x):
        inv = lax.rsqrt(jnp.mean(x * x, axis=-1, keepdims=True) + norm_eps)
        return x * inv, inv

    def rot(x, direction):
        turned = pltpu.roll(x, head // 2, axis=1) * sin
        return x * cos + turned if direction > 0 else x * cos - turned

    count = jnp.sum(valid, axis=0, keepdims=True)
    count = jnp.broadcast_to(jnp.concatenate([count, count], axis=1), (pad - cap, 2 * head))
    for t in range(heads_k):
        cols = pl.ds(t * head, head)
        unit, inv = normed(k_ref[:, cols].astype(F32))
        kunit[t] = unit
        kinv[t] = jnp.broadcast_to(inv, (cap, head))
        skv[t, 0:cap, 0:head] = rot(unit * gain_k, 1).astype(BF16)
        skv[t, 0:cap, head:] = v_ref[:, cols]
        skv[t, cap:, :] = count.astype(BF16)

    pl.semaphore_wait(barrier, len(peers))

    kv_copies = []
    for o in order:
        copy = remote(skv.at[mate[o]], rkv.at[g], kv_s.at[o], kv_r.at[o], ctx=plane[o])
        copy.start()
        kv_copies.append(copy)
    rkv[g] = skv[g]

    qd_copies = []
    for o in order + (0,):
        t = mate[o]
        for j in range(group):
            cols = pl.ds(pl.multiple_of(t * gw + j * head, head), head)
            unit, inv = normed(q_ref[:, cols].astype(F32))
            qunit[t * group + j] = unit
            qinv[t * group + j] = jnp.broadcast_to(inv, (cap, head))
            turned = rot(unit * gain_q, 1).astype(BF16)
            weighted = (gate * c_ref[:, cols].astype(F32)).astype(BF16)
            dround[t * group + j] = weighted
            if o == 0:
                rqd[g, 0:cap, j * head : (j + 1) * head] = turned
                rqd[g, 0:cap, gw + j * head : gw + (j + 1) * head] = weighted
            else:
                sqd[o - 1, :, j * head : (j + 1) * head] = turned
                sqd[o - 1, :, gw + j * head : gw + (j + 1) * head] = weighted
        if o != 0:
            copy = remote(
                sqd.at[o - 1], rqd.at[g, pl.ds(0, cap)], qd_s.at[o], qd_r.at[o], ctx=plane[o]
            )
            copy.start()
            qd_copies.append(copy)
    for m in range(SEG_DEV):
        rqd[m, cap:, :] = jnp.zeros((pad - cap, 2 * gw), BF16)

    for copy in kv_copies:
        copy.wait_recv()
    wide = SEG_DEV * pad
    lane = lax.broadcasted_iota(jnp.int32, (1, wide), 1)
    member = lane // pad
    slot = (lane % pad).astype(F32)
    counts = [rkv[m, cap : cap + 16, :].astype(F32)[0:1] for m in range(SEG_DEV)]
    have = counts[0]
    base = jnp.zeros_like(have)
    run = counts[0]
    for m in range(1, SEG_DEV):
        have = jnp.where(member == m, counts[m], have)
        base = jnp.where(member == m, run, base)
        run = run + counts[m]
    place = jnp.where(slot < have, base + slot, -1.0)
    rank = lax.broadcasted_iota(jnp.int32, (sel, wide), 0).astype(F32)
    pick = jnp.where(rank == place, 1.0, 0.0).astype(BF16)
    kv_all[seg] = dot(pick, rkv[...].reshape(wide, 2 * head), NN).astype(BF16)
    z_copies = []
    for o in far:
        copy = remote(kv_all.at[seg], kv_all.at[seg], z_s.at[o], z_r.at[o], ctx=far_dev[o])
        copy.start()
        z_copies.append(copy)

    for copy in qd_copies:
        copy.wait_recv()
    qd = dot(pick, rqd[...].reshape(wide, 2 * gw), NN).astype(BF16)
    q_rows = jnp.concatenate([qd[:, j * head : (j + 1) * head] for j in range(group)], axis=0)
    d_rows = jnp.concatenate(
        [qd[:, gw + j * head : gw + (j + 1) * head] for j in range(group)], axis=0
    )
    for copy in z_copies:
        copy.wait_recv()

    total = n_seg * sel
    keys = kv_all[:, :, 0:head].reshape(total, head)
    vals = kv_all[:, :, head:].reshape(total, head)
    row = lax.broadcasted_iota(jnp.int32, (group * sel, total), 0) % sel
    col = lax.broadcasted_iota(jnp.int32, (group * sel, total), 1)
    scores = dot(q_rows, keys, NT) * scale
    scores = jnp.where(col <= row + seg * sel, scores, -jnp.inf)
    top = jnp.max(scores, axis=-1, keepdims=True)
    exps = jnp.exp(scores - top)
    probs = exps / jnp.sum(exps, axis=-1, keepdims=True)
    probs_b = probs.astype(BF16)
    attended = dot(probs_b, vals, NN).astype(BF16)
    delta = jnp.sum(d_rows.astype(F32) * attended.astype(F32), axis=-1, keepdims=True)
    dprob = dot(d_rows, vals, NT)
    dscore = (probs * (dprob - delta)).astype(BF16)
    dkv_p[:, :, 0:head] = (dot(dscore, q_rows, TN) * scale).reshape(n_seg, sel, head)
    dkv_p[:, :, head:] = dot(probs_b, d_rows, TN).reshape(n_seg, sel, head)
    dz_copies = []
    for o in far:
        copy = remote(dkv_p.at[far[o]], dkv_r.at[seg], dz_s.at[o], dz_r.at[o], ctx=far_dev[o])
        copy.start()
        dz_copies.append(copy)
    dkv_r[seg] = dkv_p[seg]

    dq = (dot(dscore, keys, NN) * scale).astype(BF16)
    back = jnp.concatenate(
        [attended[j * sel : (j + 1) * sel] for j in range(group)]
        + [dq[j * sel : (j + 1) * sel] for j in range(group)],
        axis=1,
    )
    sback[...] = dot(pick, back, TN).astype(BF16).reshape(SEG_DEV, pad, 2 * gw)
    b_copies = []
    for o in order:
        copy = remote(
            sback.at[mate[o], pl.ds(0, cap)], rback.at[g], b_s.at[o], b_r.at[o], ctx=plane[o]
        )
        copy.start()
        b_copies.append(copy)
    rback[g] = sback[g, 0:cap]

    for copy in dz_copies:
        copy.wait_recv()
    dkv = dkv_r[0]
    for s in range(1, n_seg):
        dkv = dkv + dkv_r[s]
    skb[...] = dot(pick, dkv.astype(BF16), TN).astype(BF16).reshape(SEG_DEV, pad, 2 * head)
    kb_copies = []
    for o in order:
        copy = remote(
            skb.at[mate[o], pl.ds(0, cap)], rkb.at[g], kb_s.at[o], kb_r.at[o], ctx=plane[o]
        )
        copy.start()
        kb_copies.append(copy)
    rkb[g] = skb[g, 0:cap]

    def norm_back(grad, unit, inv, gain):
        turned = rot(grad.astype(F32), -1)
        term = jnp.sum(turned * unit, axis=0, keepdims=True)
        scaled = turned * gain
        mean = jnp.mean(scaled * unit, axis=-1, keepdims=True)
        return (inv * (scaled - unit * mean)).astype(BF16), term

    term_q = jnp.zeros((1, head), F32)
    logit = jnp.zeros((cap, head), F32)
    for o, copy in zip((0, 1, 2, 3), (None, b_copies[2], b_copies[0], b_copies[1])):
        if copy is not None:
            copy.wait_recv()
        t = mate[o]
        for j in range(group):
            cols = pl.ds(pl.multiple_of(t * gw + j * head, head), head)
            att = rback[t, :, j * head : (j + 1) * head].astype(F32)
            out_ref[:, cols] = (gate * att).astype(BF16)
            logit = logit + dround[t * group + j].astype(F32) * att
            grad, term = norm_back(
                rback[t, :, gw + j * head : gw + (j + 1) * head],
                qunit[t * group + j],
                qinv[t * group + j],
                gain_q,
            )
            gq_ref[:, cols] = grad
            term_q = term_q + term
    gl_ref[...] = (1.0 - gate) * jnp.sum(logit, axis=-1, keepdims=True)

    for copy in kb_copies:
        copy.wait_recv()
    term_k = jnp.zeros((1, head), F32)
    for t in range(heads_k):
        cols = pl.ds(t * head, head)
        grad, term = norm_back(rkb[t, :, 0:head], kunit[t], kinv[t], gain_k)
        gk_ref[:, cols] = grad
        gv_ref[:, cols] = rkb[t, :, head:]
        term_k = term_k + term

    which = lax.broadcasted_iota(jnp.int32, (8, head), 0)
    terms = jnp.where(which == 0, term_q, jnp.where(which == 1, term_k, 0.0))
    last = []
    gplane[g] = terms
    stage = []
    for o in order:
        copy = remote(gplane.at[g], gplane.at[g], g_s.at[o], g_r.at[o], ctx=plane[o])
        copy.start()
        stage.append(copy)
    for copy in stage:
        copy.wait_recv()
    last += stage
    terms = gplane[0] + gplane[1] + gplane[2] + gplane[3]
    gseg[seg] = terms
    stage = []
    for o in far:
        copy = remote(gseg.at[seg], gseg.at[seg], g_s.at[3 + o], g_r.at[3 + o], ctx=far_dev[o])
        copy.start()
        stage.append(copy)
    for copy in stage:
        copy.wait_recv()
    last += stage
    terms = gseg[0]
    for s in range(1, n_seg):
        terms = terms + gseg[s]
    gdp[my_dp] = terms
    stage = []
    for o in rows_dp:
        at = 3 + n_seg - 1 + o
        copy = remote(gdp.at[my_dp], gdp.at[my_dp], g_s.at[at], g_r.at[at], dp=rows_dp[o])
        copy.start()
        stage.append(copy)
    for copy in stage:
        copy.wait_recv()
    last += stage
    terms = gdp[0]
    for s in range(1, n_dp):
        terms = terms + gdp[s]
    selected_all = n_dp * total
    over_q = 1.0 / math.sqrt(selected_all * group * heads_k)
    over_k = 1.0 / math.sqrt(selected_all * heads_k)
    gains_ref[...] = terms * jnp.where(which == 0, over_q, over_k)

    for copy in kv_copies + qd_copies + z_copies + dz_copies + b_copies + kb_copies + last:
        copy.wait_send()


def per_device(
    n_seg,
    n_dp,
    positions,
    queries,
    keys,
    values,
    router_logits,
    out_cotangent,
    query_gain,
    key_gain,
):
    cap = positions.shape[1]
    head = query_gain.shape[0]
    width_q = queries.shape[2]
    width_k = keys.shape[2]
    heads_q = width_q // head
    heads_k = width_k // head
    gw = width_q // heads_k
    sel = SEL_DEV * SEG_DEV
    pad = sel
    pos = positions[0]
    half = jnp.arange(head // 2).astype(F32)
    frequency = jnp.exp(half * (-2.0 * math.log(rope_base) / head))
    angles = pos.astype(F32)[:, None] * frequency[None, :]
    cos = jnp.cos(angles)
    sin = jnp.sin(angles)
    gating = jax.nn.sigmoid(router_logits[0])
    live = (pos >= 0).astype(F32)
    aux = jnp.stack(
        [
            jnp.concatenate([cos, cos], axis=1),
            jnp.concatenate([-sin, sin], axis=1),
            jnp.broadcast_to(gating[:, None], (cap, head)),
            jnp.broadcast_to(live[:, None], (cap, head)),
        ]
    )
    gains = jnp.stack([query_gain, key_gain])
    vmem = pl.BlockSpec(memory_space=pltpu.VMEM)
    dma = pltpu.SemaphoreType.DMA
    n_g = 4 + n_seg - 1 + n_dp
    out, gq, gk, gv, gl, gsum = pl.pallas_call(
        functools.partial(kernel, n_seg, n_dp),
        out_shape=(
            jax.ShapeDtypeStruct((cap, width_q), BF16),
            jax.ShapeDtypeStruct((cap, width_q), BF16),
            jax.ShapeDtypeStruct((cap, width_k), BF16),
            jax.ShapeDtypeStruct((cap, width_k), BF16),
            jax.ShapeDtypeStruct((cap, head), F32),
            jax.ShapeDtypeStruct((8, head), F32),
        ),
        in_specs=[vmem] * 6,
        out_specs=(vmem,) * 6,
        scratch_shapes=[
            pltpu.VMEM((SEG_DEV, pad, 2 * head), BF16),
            pltpu.VMEM((SEG_DEV, pad, 2 * head), BF16),
            pltpu.VMEM((SEG_DEV - 1, cap, 2 * gw), BF16),
            pltpu.VMEM((SEG_DEV, pad, 2 * gw), BF16),
            pltpu.VMEM((heads_q, cap, head), F32),
            pltpu.VMEM((heads_q, cap, head), F32),
            pltpu.VMEM((heads_q, cap, head), BF16),
            pltpu.VMEM((heads_k, cap, head), F32),
            pltpu.VMEM((heads_k, cap, head), F32),
            pltpu.VMEM((n_seg, sel, 2 * head), BF16),
            pltpu.VMEM((n_seg, sel, 2 * head), F32),
            pltpu.VMEM((n_seg, sel, 2 * head), F32),
            pltpu.VMEM((SEG_DEV, pad, 2 * gw), BF16),
            pltpu.VMEM((SEG_DEV, cap, 2 * gw), BF16),
            pltpu.VMEM((SEG_DEV, pad, 2 * head), BF16),
            pltpu.VMEM((SEG_DEV, cap, 2 * head), BF16),
            pltpu.VMEM((SEG_DEV, 8, head), F32),
            pltpu.VMEM((n_seg, 8, head), F32),
            pltpu.VMEM((n_dp, 8, head), F32),
            dma((SEG_DEV,)),
            dma((SEG_DEV,)),
            dma((SEG_DEV,)),
            dma((SEG_DEV,)),
            dma((n_seg,)),
            dma((n_seg,)),
            dma((n_seg,)),
            dma((n_seg,)),
            dma((SEG_DEV,)),
            dma((SEG_DEV,)),
            dma((SEG_DEV,)),
            dma((SEG_DEV,)),
            dma((n_g,)),
            dma((n_g,)),
        ],
        compiler_params=pltpu.CompilerParams(
            collective_id=0, has_side_effects=True, vmem_limit_bytes=40 * 1024 * 1024
        ),
    )(aux, queries[0], keys[0], values[0], out_cotangent[0], gains)
    return (out[None], gq[None], gk[None], gv[None], gl[:, 0][None], gsum[0], gsum[1])


def solution(mesh):
    n_seg = mesh.shape["ctx"] // SEG_DEV
    n_dp = mesh.shape["dp"]
    return jax.shard_map(
        functools.partial(per_device, n_seg, n_dp),
        mesh=mesh,
        in_specs=(
            P("dp", "ctx"),
            P("dp", "ctx", None),
            P("dp", "ctx", None),
            P("dp", "ctx", None),
            P("dp", "ctx"),
            P("dp", "ctx", None),
            P(),
            P(),
        ),
        out_specs=(
            P("dp", "ctx", None),
            P("dp", "ctx", None),
            P("dp", "ctx", None),
            P("dp", "ctx", None),
            P("dp", "ctx"),
            P(),
            P(),
        ),
        check_vma=False,
    )
```

```python
import functools
import math

import jax
import jax.numpy as jnp
import numpy as np
from jax import lax
from jax.experimental import pallas as pl
from jax.experimental.pallas import tpu as pltpu
from jax.sharding import PartitionSpec as P

SEL_DEV = 16
SEG_DEV = 4

rope_base = 1000000.0
norm_eps = 1e-06

F32 = jnp.float32
BF16 = jnp.bfloat16


def dot(a, b, dims):
    return lax.dot_general(a, b, (dims, ((), ())), preferred_element_type=F32)


NN = ((1,), (0,))
NT = ((1,), (1,))
TN = ((0,), (0,))


def kernel(
    n_seg,
    n_dp,
    pos_ref,
    logit_ref,
    q_ref,
    k_ref,
    v_ref,
    c_ref,
    gain_ref,
    out_ref,
    gq_ref,
    gk_ref,
    gv_ref,
    gl_ref,
    gains_q_ref,
    gains_k_ref,
    skv,
    rkv,
    sq,
    rq,
    sd,
    rd,
    qunit,
    qinv,
    dround,
    kunit,
    kinv,
    kv_all,
    dkv_p,
    dkv_r,
    satt,
    ratt,
    sdq,
    rdq,
    skb,
    rkb,
    gplane,
    gall,
    kv_s,
    kv_r,
    q_s,
    q_r,
    d_s,
    d_r,
    z_s,
    z_r,
    dz_s,
    dz_r,
    b_s,
    b_r,
    e_s,
    e_r,
    kb_s,
    kb_r,
    g_s,
    g_r,
):
    cap, width_q = q_ref.shape
    width_k = k_ref.shape[1]
    head = gain_ref.shape[1]
    heads_k = width_k // head
    group = width_q // width_k
    gw = group * head
    sel = SEL_DEV * SEG_DEV
    pad = rkv.shape[1]
    scale = 1.0 / math.sqrt(head)

    my_dp = lax.axis_index("dp")
    my_ctx = lax.axis_index("ctx")
    seg = my_ctx // SEG_DEV
    g = my_ctx % SEG_DEV
    mate = {0: g, 1: g + 1 - 2 * (g % 2), 2: (g + 2) % 4, 3: 3 - g}
    plane = {o: seg * SEG_DEV + mate[o] for o in (1, 2, 3)}
    far = {o: (seg + o) % n_seg for o in range(1, n_seg)}
    far_dev = {o: far[o] * SEG_DEV + g for o in far}
    cells = n_dp * n_seg
    cell = my_dp * n_seg + seg
    others = {o: (cell + o) % cells for o in range(1, cells)}
    order = (2, 3, 1)

    def remote(src, dst, ssem, rsem, ctx=None, dp=None):
        return pltpu.make_async_remote_copy(
            src_ref=src,
            dst_ref=dst,
            send_sem=ssem,
            recv_sem=rsem,
            device_id=(my_dp if dp is None else dp, my_ctx if ctx is None else ctx),
            device_id_type=pl.DeviceIdType.MESH,
        )

    barrier = pltpu.get_barrier_semaphore()
    peers = [(my_dp, plane[o]) for o in order]
    peers += [(c // n_seg, c % n_seg * SEG_DEV + g) for c in others.values()]
    for peer in peers:
        pl.semaphore_signal(barrier, inc=1, device_id=peer, device_id_type=pl.DeviceIdType.MESH)

    eye = lax.broadcasted_iota(jnp.int32, (cap, cap), 0) == lax.broadcasted_iota(
        jnp.int32, (cap, cap), 1
    )

    def column(line):
        return jnp.sum(jnp.where(eye, line, 0.0), axis=1, keepdims=True)

    pos = jnp.broadcast_to(column(pos_ref[...].astype(F32)), (cap, head))
    valid = jnp.where(pos >= 0.0, 1.0, 0.0)
    angle = pos * gain_ref[2:3]
    cos = jnp.cos(angle)
    sin = jnp.sin(angle)
    sin = jnp.where(lax.broadcasted_iota(jnp.int32, (cap, head), 1) < head // 2, -sin, sin)
    gate = jax.nn.sigmoid(jnp.broadcast_to(column(logit_ref[...]), (cap, head)))
    gain_q = gain_ref[0:1]
    gain_k = gain_ref[1:2]

    def normed(x):
        inv = lax.rsqrt(jnp.mean(x * x, axis=-1, keepdims=True) + norm_eps)
        return x * inv, inv

    def rot(x, direction):
        turned = pltpu.roll(x, head // 2, axis=1) * sin
        return x * cos + turned if direction > 0 else x * cos - turned

    count = jnp.sum(valid, axis=0, keepdims=True)
    count = jnp.broadcast_to(jnp.concatenate([count, count], axis=1), (pad - cap, 2 * head))
    for t in range(heads_k):
        cols = pl.ds(t * head, head)
        unit, inv = normed(k_ref[:, cols].astype(F32))
        kunit[t] = unit
        kinv[t] = jnp.broadcast_to(inv, (cap, head))
        skv[t, 0:cap, 0:head] = rot(unit * gain_k, 1).astype(BF16)
        skv[t, 0:cap, head:] = v_ref[:, cols]
        skv[t, cap:, :] = count.astype(BF16)

    pl.semaphore_wait(barrier, len(peers))

    kv_copies = []
    for o in order:
        copy = remote(skv.at[mate[o]], rkv.at[g], kv_s.at[o], kv_r.at[o], ctx=plane[o])
        copy.start()
        kv_copies.append(copy)
    rkv[g] = skv[g]

    q_copies = []
    d_copies = []
    for o in order + (0,):
        t = mate[o]
        for j in range(group):
            cols = pl.ds(pl.multiple_of(t * gw + j * head, head), head)
            unit, inv = normed(q_ref[:, cols].astype(F32))
            qunit[t * group + j] = unit
            qinv[t * group + j] = jnp.broadcast_to(inv, (cap, head))
            turned = rot(unit * gain_q, 1).astype(BF16)
            if o == 0:
                rq[g, 0:cap, j * head : (j + 1) * head] = turned
            else:
                sq[o - 1, :, j * head : (j + 1) * head] = turned
        if o != 0:
            copy = remote(
                sq.at[o - 1], rq.at[g, pl.ds(0, cap)], q_s.at[o], q_r.at[o], ctx=plane[o]
            )
            copy.start()
            q_copies.append(copy)
    for o in order + (0,):
        t = mate[o]
        for j in range(group):
            cols = pl.ds(pl.multiple_of(t * gw + j * head, head), head)
            weighted = (gate * c_ref[:, cols].astype(F32)).astype(BF16)
            dround[t * group + j] = weighted
            if o == 0:
                rd[g, 0:cap, j * head : (j + 1) * head] = weighted
            else:
                sd[o - 1, :, j * head : (j + 1) * head] = weighted
        if o != 0:
            copy = remote(
                sd.at[o - 1], rd.at[g, pl.ds(0, cap)], d_s.at[o], d_r.at[o], ctx=plane[o]
            )
            copy.start()
            d_copies.append(copy)
    for m in range(SEG_DEV):
        rq[m, cap:, :] = jnp.zeros((pad - cap, gw), BF16)
        rd[m, cap:, :] = jnp.zeros((pad - cap, gw), BF16)

    for copy in kv_copies:
        copy.wait_recv()
    wide = SEG_DEV * pad
    lane = lax.broadcasted_iota(jnp.int32, (1, wide), 1)
    member = lane // pad
    slot = (lane % pad).astype(F32)
    counts = [rkv[m, cap : cap + 16, :].astype(F32)[0:1] for m in range(SEG_DEV)]
    have = counts[0]
    base = jnp.zeros_like(have)
    run = counts[0]
    for m in range(1, SEG_DEV):
        have = jnp.where(member == m, counts[m], have)
        base = jnp.where(member == m, run, base)
        run = run + counts[m]
    place = jnp.where(slot < have, base + slot, -1.0)
    rank = lax.broadcasted_iota(jnp.int32, (sel, wide), 0).astype(F32)
    pick = jnp.where(rank == place, 1.0, 0.0).astype(BF16)
    kv_all[seg] = dot(pick, rkv[...].reshape(wide, 2 * head), NN).astype(BF16)
    z_copies = []
    for o in far:
        copy = remote(kv_all.at[seg], kv_all.at[seg], z_s.at[o], z_r.at[o], ctx=far_dev[o])
        copy.start()
        z_copies.append(copy)

    def heads_down(wide_rows):
        return jnp.concatenate(
            [wide_rows[:, j * head : (j + 1) * head] for j in range(group)], axis=0
        )

    def heads_across(tall_rows):
        return jnp.concatenate([tall_rows[j * sel : (j + 1) * sel] for j in range(group)], axis=1)

    for copy in q_copies:
        copy.wait_recv()
    q_rows = heads_down(dot(pick, rq[...].reshape(wide, gw), NN).astype(BF16))
    for copy in z_copies:
        copy.wait_recv()

    total = n_seg * sel
    keys = kv_all[:, :, 0:head].reshape(total, head)
    vals = kv_all[:, :, head:].reshape(total, head)
    row = lax.broadcasted_iota(jnp.int32, (group * sel, total), 0) % sel
    col = lax.broadcasted_iota(jnp.int32, (group * sel, total), 1)
    scores = dot(q_rows, keys, NT) * scale
    scores = jnp.where(col <= row + seg * sel, scores, -jnp.inf)
    top = jnp.max(scores, axis=-1, keepdims=True)
    exps = jnp.exp(scores - top)
    probs = exps / jnp.sum(exps, axis=-1, keepdims=True)
    probs_b = probs.astype(BF16)
    attended = dot(probs_b, vals, NN).astype(BF16)
    satt[...] = dot(pick, heads_across(attended), TN).astype(BF16).reshape(SEG_DEV, pad, gw)
    b_copies = []
    for o in order:
        copy = remote(
            satt.at[mate[o], pl.ds(0, cap)], ratt.at[g], b_s.at[o], b_r.at[o], ctx=plane[o]
        )
        copy.start()
        b_copies.append(copy)
    ratt[g] = satt[g, 0:cap]

    for copy in d_copies:
        copy.wait_recv()
    d_rows = heads_down(dot(pick, rd[...].reshape(wide, gw), NN).astype(BF16))
    delta = jnp.sum(d_rows.astype(F32) * attended.astype(F32), axis=-1, keepdims=True)
    dprob = dot(d_rows, vals, NT)
    dscore = (probs * (dprob - delta)).astype(BF16)
    dkv_p[:, :, 0:head] = (dot(dscore, q_rows, TN) * scale).reshape(n_seg, sel, head)
    dkv_p[:, :, head:] = dot(probs_b, d_rows, TN).reshape(n_seg, sel, head)
    dz_copies = []
    for o in far:
        copy = remote(dkv_p.at[far[o]], dkv_r.at[seg], dz_s.at[o], dz_r.at[o], ctx=far_dev[o])
        copy.start()
        dz_copies.append(copy)
    dkv_r[seg] = dkv_p[seg]

    dq = (dot(dscore, keys, NN) * scale).astype(BF16)
    sdq[...] = dot(pick, heads_across(dq), TN).astype(BF16).reshape(SEG_DEV, pad, gw)
    e_copies = []
    for o in order:
        copy = remote(
            sdq.at[mate[o], pl.ds(0, cap)], rdq.at[g], e_s.at[o], e_r.at[o], ctx=plane[o]
        )
        copy.start()
        e_copies.append(copy)
    rdq[g] = sdq[g, 0:cap]

    logit = jnp.zeros((cap, head), F32)
    for copy in b_copies:
        copy.wait_recv()
    for t in range(SEG_DEV):
        for j in range(group):
            cols = pl.ds(t * gw + j * head, head)
            att = ratt[t, :, j * head : (j + 1) * head].astype(F32)
            out_ref[:, cols] = (gate * att).astype(BF16)
            logit = logit + dround[t * group + j].astype(F32) * att
    total_logit = (1.0 - gate[:, 0:1]) * jnp.sum(logit, axis=-1, keepdims=True)
    gl_ref[...] = jnp.sum(jnp.where(eye, total_logit, 0.0), axis=0, keepdims=True)

    def norm_back(grad, unit, inv, gain):
        turned = rot(grad.astype(F32), -1)
        term = jnp.sum(turned * unit, axis=0, keepdims=True)
        scaled = turned * gain
        mean = jnp.mean(scaled * unit, axis=-1, keepdims=True)
        return (inv * (scaled - unit * mean)).astype(BF16), term

    def query_back(o, term_q):
        t = mate[o]
        for j in range(group):
            cols = pl.ds(pl.multiple_of(t * gw + j * head, head), head)
            grad, term = norm_back(
                rdq[t, :, j * head : (j + 1) * head],
                qunit[t * group + j],
                qinv[t * group + j],
                gain_q,
            )
            gq_ref[:, cols] = grad
            term_q = term_q + term
        return term_q

    term_q = query_back(0, jnp.zeros((1, head), F32))

    for copy in dz_copies:
        copy.wait_recv()
    dkv = dkv_r[0]
    for s in range(1, n_seg):
        dkv = dkv + dkv_r[s]
    skb[...] = dot(pick, dkv.astype(BF16), TN).astype(BF16).reshape(SEG_DEV, pad, 2 * head)
    kb_copies = []
    for o in order:
        copy = remote(
            skb.at[mate[o], pl.ds(0, cap)], rkb.at[g], kb_s.at[o], kb_r.at[o], ctx=plane[o]
        )
        copy.start()
        kb_copies.append(copy)
    rkb[g] = skb[g, 0:cap]

    for o, copy in zip((1, 2, 3), (e_copies[2], e_copies[0], e_copies[1])):
        copy.wait_recv()
        term_q = query_back(o, term_q)

    for copy in kb_copies:
        copy.wait_recv()
    term_k = jnp.zeros((1, head), F32)
    for t in range(heads_k):
        cols = pl.ds(t * head, head)
        grad, term = norm_back(rkb[t, :, 0:head], kunit[t], kinv[t], gain_k)
        gk_ref[:, cols] = grad
        gv_ref[:, cols] = rkb[t, :, head:]
        term_k = term_k + term

    which = lax.broadcasted_iota(jnp.int32, (8, head), 0)
    terms = jnp.where(which == 0, term_q, jnp.where(which == 1, term_k, 0.0))
    last = []
    gplane[g] = terms
    stage = []
    for o in order:
        copy = remote(gplane.at[g], gplane.at[g], g_s.at[o], g_r.at[o], ctx=plane[o])
        copy.start()
        stage.append(copy)
    for copy in stage:
        copy.wait_recv()
    last += stage
    terms = gplane[0] + gplane[1] + gplane[2] + gplane[3]
    gall[cell] = terms
    stage = []
    for o, c in others.items():
        copy = remote(
            gall.at[cell],
            gall.at[cell],
            g_s.at[3 + o],
            g_r.at[3 + o],
            ctx=c % n_seg * SEG_DEV + g,
            dp=c // n_seg,
        )
        copy.start()
        stage.append(copy)
    for copy in stage:
        copy.wait_recv()
    last += stage
    terms = gall[0]
    for s in range(1, cells):
        terms = terms + gall[s]
    selected_all = n_dp * total
    over_q = 1.0 / math.sqrt(selected_all * group * heads_k)
    over_k = 1.0 / math.sqrt(selected_all * heads_k)
    gains_q_ref[...] = terms[0:1] * over_q
    gains_k_ref[...] = terms[1:2] * over_k

    mine = kv_copies + q_copies + d_copies + z_copies + dz_copies
    for copy in mine + b_copies + e_copies + kb_copies + last:
        copy.wait_send()


def place_results(*refs):
    sems = refs[-1]
    half = len(refs) // 2
    copies = [
        pltpu.make_async_copy(refs[i], refs[half + i], sems.at[i]) for i in range(half)
    ]
    for copy in copies:
        copy.start()
    for copy in copies:
        copy.wait()


def per_device(
    n_seg,
    n_dp,
    positions,
    queries,
    keys,
    values,
    router_logits,
    out_cotangent,
    query_gain,
    key_gain,
):
    cap = positions.shape[1]
    head = query_gain.shape[0]
    width_q = queries.shape[2]
    width_k = keys.shape[2]
    heads_q = width_q // head
    heads_k = width_k // head
    gw = width_q // heads_k
    sel = SEL_DEV * SEG_DEV
    pad = sel
    steps = np.arange(head // 2, dtype=np.float64) * (-2.0 * math.log(rope_base) / head)
    frequency = np.tile(np.exp(steps), 2).astype(np.float32)
    gains = jnp.stack([query_gain, key_gain, jnp.asarray(frequency)])
    vmem = pl.BlockSpec(memory_space=pltpu.VMEM)
    dma = pltpu.SemaphoreType.DMA
    n_g = 3 + n_seg * n_dp
    results = pl.pallas_call(
        functools.partial(kernel, n_seg, n_dp),
        out_shape=(
            jax.ShapeDtypeStruct((cap, width_q), BF16),
            jax.ShapeDtypeStruct((cap, width_q), BF16),
            jax.ShapeDtypeStruct((cap, width_k), BF16),
            jax.ShapeDtypeStruct((cap, width_k), BF16),
            jax.ShapeDtypeStruct((1, cap), F32),
            jax.ShapeDtypeStruct((1, head), F32),
            jax.ShapeDtypeStruct((1, head), F32),
        ),
        in_specs=[vmem] * 7,
        out_specs=(vmem,) * 7,
        scratch_shapes=[
            pltpu.VMEM((SEG_DEV, pad, 2 * head), BF16),
            pltpu.VMEM((SEG_DEV, pad, 2 * head), BF16),
            pltpu.VMEM((SEG_DEV - 1, cap, gw), BF16),
            pltpu.VMEM((SEG_DEV, pad, gw), BF16),
            pltpu.VMEM((SEG_DEV - 1, cap, gw), BF16),
            pltpu.VMEM((SEG_DEV, pad, gw), BF16),
            pltpu.VMEM((heads_q, cap, head), F32),
            pltpu.VMEM((heads_q, cap, head), F32),
            pltpu.VMEM((heads_q, cap, head), BF16),
            pltpu.VMEM((heads_k, cap, head), F32),
            pltpu.VMEM((heads_k, cap, head), F32),
            pltpu.VMEM((n_seg, sel, 2 * head), BF16),
            pltpu.VMEM((n_seg, sel, 2 * head), F32),
            pltpu.VMEM((n_seg, sel, 2 * head), F32),
            pltpu.VMEM((SEG_DEV, pad, gw), BF16),
            pltpu.VMEM((SEG_DEV, cap, gw), BF16),
            pltpu.VMEM((SEG_DEV, pad, gw), BF16),
            pltpu.VMEM((SEG_DEV, cap, gw), BF16),
            pltpu.VMEM((SEG_DEV, pad, 2 * head), BF16),
            pltpu.VMEM((SEG_DEV, cap, 2 * head), BF16),
            pltpu.VMEM((SEG_DEV, 8, head), F32),
            pltpu.VMEM((n_seg * n_dp, 8, head), F32),
            dma((SEG_DEV,)),
            dma((SEG_DEV,)),
            dma((SEG_DEV,)),
            dma((SEG_DEV,)),
            dma((SEG_DEV,)),
            dma((SEG_DEV,)),
            dma((n_seg,)),
            dma((n_seg,)),
            dma((n_seg,)),
            dma((n_seg,)),
            dma((SEG_DEV,)),
            dma((SEG_DEV,)),
            dma((SEG_DEV,)),
            dma((SEG_DEV,)),
            dma((SEG_DEV,)),
            dma((SEG_DEV,)),
            dma((n_g,)),
            dma((n_g,)),
        ],
        compiler_params=pltpu.CompilerParams(
            collective_id=0, has_side_effects=True, vmem_limit_bytes=40 * 1024 * 1024
        ),
    )(positions, router_logits, queries[0], keys[0], values[0], out_cotangent[0], gains)
    count = len(results)
    anywhere = pl.BlockSpec(memory_space=pl.ANY)
    out, gq, gk, gv, gl, gain_q, gain_k = pl.pallas_call(
        place_results,
        out_shape=tuple(jax.ShapeDtypeStruct(r.shape, r.dtype) for r in results),
        in_specs=[anywhere] * count,
        out_specs=(anywhere,) * count,
        scratch_shapes=[dma((count,))],
    )(*results)
    return (
        out[None],
        gq[None],
        gk[None],
        gv[None],
        gl,
        gain_q.reshape(head),
        gain_k.reshape(head),
    )


def solution(mesh):
    n_seg = mesh.shape["ctx"] // SEG_DEV
    n_dp = mesh.shape["dp"]
    return jax.shard_map(
        functools.partial(per_device, n_seg, n_dp),
        mesh=mesh,
        in_specs=(
            P("dp", "ctx"),
            P("dp", "ctx", None),
            P("dp", "ctx", None),
            P("dp", "ctx", None),
            P("dp", "ctx"),
            P("dp", "ctx", None),
            P(),
            P(),
        ),
        out_specs=(
            P("dp", "ctx", None),
            P("dp", "ctx", None),
            P("dp", "ctx", None),
            P("dp", "ctx", None),
            P("dp", "ctx"),
            P(),
            P(),
        ),
        check_vma=False,
    )
```

```python
import functools
import math

import jax
import jax.numpy as jnp
import numpy as np
from jax import lax
from jax.experimental import pallas as pl
from jax.experimental.pallas import tpu as pltpu
from jax.sharding import PartitionSpec as P

SEL_DEV = 16
SEG_DEV = 4

rope_base = 1000000.0
norm_eps = 1e-06

F32 = jnp.float32
BF16 = jnp.bfloat16


def dot(a, b, dims):
    return lax.dot_general(a, b, (dims, ((), ())), preferred_element_type=F32)


NN = ((1,), (0,))
NT = ((1,), (1,))
TN = ((0,), (0,))


def kernel(
    n_seg,
    n_dp,
    pos_hbm,
    logit_hbm,
    q_hbm,
    k_hbm,
    v_hbm,
    c_hbm,
    gq_in_hbm,
    gk_in_hbm,
    freq_hbm,
    out_ref,
    gq_ref,
    gk_ref,
    gv_ref,
    gl_ref,
    gains_q_ref,
    gains_k_ref,
    pos_ref,
    logit_ref,
    q_ref,
    k_ref,
    v_ref,
    c_ref,
    gq_in_ref,
    gk_in_ref,
    freq_ref,
    in_s,
    skv,
    rkv,
    sq,
    rq,
    sd,
    rd,
    qunit,
    qinv,
    dround,
    kunit,
    kinv,
    kv_all,
    dkv_p,
    dkv_r,
    satt,
    ratt,
    sdq,
    rdq,
    skb,
    rkb,
    gplane,
    gall,
    kv_s,
    kv_r,
    q_s,
    q_r,
    d_s,
    d_r,
    z_s,
    z_r,
    dz_s,
    dz_r,
    b_s,
    b_r,
    e_s,
    e_r,
    kb_s,
    kb_r,
    g_s,
    g_r,
):
    given = (
        (pos_hbm, pos_ref),
        (logit_hbm, logit_ref),
        (freq_hbm, freq_ref),
        (gk_in_hbm, gk_in_ref),
        (k_hbm, k_ref),
        (v_hbm, v_ref),
        (gq_in_hbm, gq_in_ref),
        (q_hbm, q_ref),
        (c_hbm, c_ref),
    )
    loads = [pltpu.make_async_copy(a, b, in_s.at[i]) for i, (a, b) in enumerate(given)]
    for load in loads:
        load.start()
    cap, width_q = q_ref.shape
    width_k = k_ref.shape[1]
    head = freq_ref.shape[1]
    heads_k = width_k // head
    group = width_q // width_k
    gw = group * head
    sel = SEL_DEV * SEG_DEV
    pad = rkv.shape[1]
    scale = 1.0 / math.sqrt(head)

    my_dp = lax.axis_index("dp")
    my_ctx = lax.axis_index("ctx")
    seg = my_ctx // SEG_DEV
    g = my_ctx % SEG_DEV
    mate = {0: g, 1: g + 1 - 2 * (g % 2), 2: (g + 2) % 4, 3: 3 - g}
    plane = {o: seg * SEG_DEV + mate[o] for o in (1, 2, 3)}
    far = {o: (seg + o) % n_seg for o in range(1, n_seg)}
    far_dev = {o: far[o] * SEG_DEV + g for o in far}
    cells = n_dp * n_seg
    cell = my_dp * n_seg + seg
    others = {o: (cell + o) % cells for o in range(1, cells)}
    order = (2, 3, 1)

    def remote(src, dst, ssem, rsem, ctx=None, dp=None):
        return pltpu.make_async_remote_copy(
            src_ref=src,
            dst_ref=dst,
            send_sem=ssem,
            recv_sem=rsem,
            device_id=(my_dp if dp is None else dp, my_ctx if ctx is None else ctx),
            device_id_type=pl.DeviceIdType.MESH,
        )

    barrier = pltpu.get_barrier_semaphore()
    peers = [(my_dp, plane[o]) for o in order]
    peers += [(c // n_seg, c % n_seg * SEG_DEV + g) for c in others.values()]
    for peer in peers:
        pl.semaphore_signal(barrier, inc=1, device_id=peer, device_id_type=pl.DeviceIdType.MESH)

    eye = lax.broadcasted_iota(jnp.int32, (cap, cap), 0) == lax.broadcasted_iota(
        jnp.int32, (cap, cap), 1
    )

    def column(line):
        return jnp.sum(jnp.where(eye, line, 0.0), axis=1, keepdims=True)

    for load in loads[:6]:
        load.wait()
    pos = jnp.broadcast_to(column(pos_ref[...].astype(F32)), (cap, head))
    valid = jnp.where(pos >= 0.0, 1.0, 0.0)
    angle = pos * freq_ref[...]
    cos = jnp.cos(angle)
    sin = jnp.sin(angle)
    sin = jnp.where(lax.broadcasted_iota(jnp.int32, (cap, head), 1) < head // 2, -sin, sin)
    gate = jax.nn.sigmoid(jnp.broadcast_to(column(logit_ref[...]), (cap, head)))
    gain_k = gk_in_ref[...]

    def normed(x):
        inv = lax.rsqrt(jnp.mean(x * x, axis=-1, keepdims=True) + norm_eps)
        return x * inv, inv

    def rot(x, direction):
        turned = pltpu.roll(x, head // 2, axis=1) * sin
        return x * cos + turned if direction > 0 else x * cos - turned

    count = jnp.sum(valid, axis=0, keepdims=True)
    count = jnp.broadcast_to(jnp.concatenate([count, count], axis=1), (pad - cap, 2 * head))
    for t in range(heads_k):
        cols = pl.ds(t * head, head)
        unit, inv = normed(k_ref[:, cols].astype(F32))
        kunit[t] = unit
        kinv[t] = jnp.broadcast_to(inv, (cap, head))
        skv[t, 0:cap, 0:head] = rot(unit * gain_k, 1).astype(BF16)
        skv[t, 0:cap, head:] = v_ref[:, cols]
        skv[t, cap:, :] = count.astype(BF16)

    pl.semaphore_wait(barrier, len(peers))

    kv_copies = []
    for o in order:
        copy = remote(skv.at[mate[o]], rkv.at[g], kv_s.at[o], kv_r.at[o], ctx=plane[o])
        copy.start()
        kv_copies.append(copy)
    rkv[g] = skv[g]

    q_copies = []
    d_copies = []
    for load in loads[6:8]:
        load.wait()
    gain_q = gq_in_ref[...]
    for o in order + (0,):
        t = mate[o]
        for j in range(group):
            cols = pl.ds(pl.multiple_of(t * gw + j * head, head), head)
            unit, inv = normed(q_ref[:, cols].astype(F32))
            qunit[t * group + j] = unit
            qinv[t * group + j] = jnp.broadcast_to(inv, (cap, head))
            turned = rot(unit * gain_q, 1).astype(BF16)
            if o == 0:
                rq[g, 0:cap, j * head : (j + 1) * head] = turned
            else:
                sq[o - 1, :, j * head : (j + 1) * head] = turned
        if o != 0:
            copy = remote(
                sq.at[o - 1], rq.at[g, pl.ds(0, cap)], q_s.at[o], q_r.at[o], ctx=plane[o]
            )
            copy.start()
            q_copies.append(copy)
    loads[8].wait()
    for o in order + (0,):
        t = mate[o]
        for j in range(group):
            cols = pl.ds(pl.multiple_of(t * gw + j * head, head), head)
            weighted = (gate * c_ref[:, cols].astype(F32)).astype(BF16)
            dround[t * group + j] = weighted
            if o == 0:
                rd[g, 0:cap, j * head : (j + 1) * head] = weighted
            else:
                sd[o - 1, :, j * head : (j + 1) * head] = weighted
        if o != 0:
            copy = remote(
                sd.at[o - 1], rd.at[g, pl.ds(0, cap)], d_s.at[o], d_r.at[o], ctx=plane[o]
            )
            copy.start()
            d_copies.append(copy)
    for m in range(SEG_DEV):
        rq[m, cap:, :] = jnp.zeros((pad - cap, gw), BF16)
        rd[m, cap:, :] = jnp.zeros((pad - cap, gw), BF16)

    for copy in kv_copies:
        copy.wait_recv()
    wide = SEG_DEV * pad
    lane = lax.broadcasted_iota(jnp.int32, (1, wide), 1)
    member = lane // pad
    slot = (lane % pad).astype(F32)
    counts = [rkv[m, cap : cap + 16, :].astype(F32)[0:1] for m in range(SEG_DEV)]
    have = counts[0]
    base = jnp.zeros_like(have)
    run = counts[0]
    for m in range(1, SEG_DEV):
        have = jnp.where(member == m, counts[m], have)
        base = jnp.where(member == m, run, base)
        run = run + counts[m]
    place = jnp.where(slot < have, base + slot, -1.0)
    rank = lax.broadcasted_iota(jnp.int32, (sel, wide), 0).astype(F32)
    pick = jnp.where(rank == place, 1.0, 0.0).astype(BF16)
    kv_all[seg] = dot(pick, rkv[...].reshape(wide, 2 * head), NN).astype(BF16)
    z_copies = []
    for o in far:
        copy = remote(kv_all.at[seg], kv_all.at[seg], z_s.at[o], z_r.at[o], ctx=far_dev[o])
        copy.start()
        z_copies.append(copy)

    def heads_down(wide_rows):
        return jnp.concatenate(
            [wide_rows[:, j * head : (j + 1) * head] for j in range(group)], axis=0
        )

    def heads_across(tall_rows):
        return jnp.concatenate([tall_rows[j * sel : (j + 1) * sel] for j in range(group)], axis=1)

    for copy in q_copies:
        copy.wait_recv()
    q_rows = heads_down(dot(pick, rq[...].reshape(wide, gw), NN).astype(BF16))
    for copy in z_copies:
        copy.wait_recv()

    total = n_seg * sel
    keys = kv_all[:, :, 0:head].reshape(total, head)
    vals = kv_all[:, :, head:].reshape(total, head)
    row = lax.broadcasted_iota(jnp.int32, (group * sel, total), 0) % sel
    col = lax.broadcasted_iota(jnp.int32, (group * sel, total), 1)
    scores = dot(q_rows, keys, NT) * scale
    scores = jnp.where(col <= row + seg * sel, scores, -jnp.inf)
    top = jnp.max(scores, axis=-1, keepdims=True)
    exps = jnp.exp(scores - top)
    probs = exps / jnp.sum(exps, axis=-1, keepdims=True)
    probs_b = probs.astype(BF16)
    attended = dot(probs_b, vals, NN).astype(BF16)
    satt[...] = dot(pick, heads_across(attended), TN).astype(BF16).reshape(SEG_DEV, pad, gw)
    b_copies = []
    for o in order:
        copy = remote(
            satt.at[mate[o], pl.ds(0, cap)], ratt.at[g], b_s.at[o], b_r.at[o], ctx=plane[o]
        )
        copy.start()
        b_copies.append(copy)
    ratt[g] = satt[g, 0:cap]

    for copy in d_copies:
        copy.wait_recv()
    d_rows = heads_down(dot(pick, rd[...].reshape(wide, gw), NN).astype(BF16))
    delta = jnp.sum(d_rows.astype(F32) * attended.astype(F32), axis=-1, keepdims=True)
    dprob = dot(d_rows, vals, NT)
    dscore = (probs * (dprob - delta)).astype(BF16)
    dkv_p[:, :, 0:head] = (dot(dscore, q_rows, TN) * scale).reshape(n_seg, sel, head)
    dkv_p[:, :, head:] = dot(probs_b, d_rows, TN).reshape(n_seg, sel, head)
    dz_copies = []
    for o in far:
        copy = remote(dkv_p.at[far[o]], dkv_r.at[seg], dz_s.at[o], dz_r.at[o], ctx=far_dev[o])
        copy.start()
        dz_copies.append(copy)
    dkv_r[seg] = dkv_p[seg]

    dq = (dot(dscore, keys, NN) * scale).astype(BF16)
    sdq[...] = dot(pick, heads_across(dq), TN).astype(BF16).reshape(SEG_DEV, pad, gw)
    e_copies = []
    for o in order:
        copy = remote(
            sdq.at[mate[o], pl.ds(0, cap)], rdq.at[g], e_s.at[o], e_r.at[o], ctx=plane[o]
        )
        copy.start()
        e_copies.append(copy)
    rdq[g] = sdq[g, 0:cap]

    logit = jnp.zeros((cap, head), F32)
    for copy in b_copies:
        copy.wait_recv()
    for t in range(SEG_DEV):
        for j in range(group):
            cols = pl.ds(t * gw + j * head, head)
            att = ratt[t, :, j * head : (j + 1) * head].astype(F32)
            out_ref[:, cols] = (gate * att).astype(BF16)
            logit = logit + dround[t * group + j].astype(F32) * att
    total_logit = (1.0 - gate[:, 0:1]) * jnp.sum(logit, axis=-1, keepdims=True)
    gl_ref[...] = jnp.sum(jnp.where(eye, total_logit, 0.0), axis=0, keepdims=True)

    def norm_back(grad, unit, inv, gain):
        turned = rot(grad.astype(F32), -1)
        term = jnp.sum(turned * unit, axis=0, keepdims=True)
        scaled = turned * gain
        mean = jnp.mean(scaled * unit, axis=-1, keepdims=True)
        return (inv * (scaled - unit * mean)).astype(BF16), term

    def query_back(o, term_q):
        t = mate[o]
        for j in range(group):
            cols = pl.ds(pl.multiple_of(t * gw + j * head, head), head)
            grad, term = norm_back(
                rdq[t, :, j * head : (j + 1) * head],
                qunit[t * group + j],
                qinv[t * group + j],
                gain_q,
            )
            gq_ref[:, cols] = grad
            term_q = term_q + term
        return term_q

    term_q = query_back(0, jnp.zeros((1, head), F32))

    for copy in dz_copies:
        copy.wait_recv()
    dkv = dkv_r[0]
    for s in range(1, n_seg):
        dkv = dkv + dkv_r[s]
    skb[...] = dot(pick, dkv.astype(BF16), TN).astype(BF16).reshape(SEG_DEV, pad, 2 * head)
    kb_copies = []
    for o in order:
        copy = remote(
            skb.at[mate[o], pl.ds(0, cap)], rkb.at[g], kb_s.at[o], kb_r.at[o], ctx=plane[o]
        )
        copy.start()
        kb_copies.append(copy)
    rkb[g] = skb[g, 0:cap]

    for o, copy in zip((1, 2, 3), (e_copies[2], e_copies[0], e_copies[1])):
        copy.wait_recv()
        term_q = query_back(o, term_q)

    for copy in kb_copies:
        copy.wait_recv()
    term_k = jnp.zeros((1, head), F32)
    for t in range(heads_k):
        cols = pl.ds(t * head, head)
        grad, term = norm_back(rkb[t, :, 0:head], kunit[t], kinv[t], gain_k)
        gk_ref[:, cols] = grad
        gv_ref[:, cols] = rkb[t, :, head:]
        term_k = term_k + term

    which = lax.broadcasted_iota(jnp.int32, (8, head), 0)
    terms = jnp.where(which == 0, term_q, jnp.where(which == 1, term_k, 0.0))
    last = []
    gplane[g] = terms
    stage = []
    for o in order:
        copy = remote(gplane.at[g], gplane.at[g], g_s.at[o], g_r.at[o], ctx=plane[o])
        copy.start()
        stage.append(copy)
    for copy in stage:
        copy.wait_recv()
    last += stage
    terms = gplane[0] + gplane[1] + gplane[2] + gplane[3]
    gall[cell] = terms
    stage = []
    for o, c in others.items():
        copy = remote(
            gall.at[cell],
            gall.at[cell],
            g_s.at[3 + o],
            g_r.at[3 + o],
            ctx=c % n_seg * SEG_DEV + g,
            dp=c // n_seg,
        )
        copy.start()
        stage.append(copy)
    for copy in stage:
        copy.wait_recv()
    last += stage
    terms = gall[0]
    for s in range(1, cells):
        terms = terms + gall[s]
    selected_all = n_dp * total
    over_q = 1.0 / math.sqrt(selected_all * group * heads_k)
    over_k = 1.0 / math.sqrt(selected_all * heads_k)
    gains_q_ref[...] = terms[0:1] * over_q
    gains_k_ref[...] = terms[1:2] * over_k

    mine = kv_copies + q_copies + d_copies + z_copies + dz_copies
    for copy in mine + b_copies + e_copies + kb_copies + last:
        copy.wait_send()


def place_results(*refs):
    count = (len(refs) - 2) // 3
    given, placed, held = (refs[i * count : (i + 1) * count] for i in range(3))
    load_s, store_s = refs[-2:]
    loads = [pltpu.make_async_copy(given[i], held[i], load_s.at[i]) for i in range(count)]
    stores = [pltpu.make_async_copy(held[i], placed[i], store_s.at[i]) for i in range(count)]
    for load in loads:
        load.start()
    for load, store in zip(loads, stores):
        load.wait()
        store.start()
    for store in stores:
        store.wait()


def per_device(
    n_seg,
    n_dp,
    positions,
    queries,
    keys,
    values,
    router_logits,
    out_cotangent,
    query_gain,
    key_gain,
):
    cap = positions.shape[1]
    head = query_gain.shape[0]
    width_q = queries.shape[2]
    width_k = keys.shape[2]
    heads_q = width_q // head
    heads_k = width_k // head
    gw = width_q // heads_k
    sel = SEL_DEV * SEG_DEV
    pad = sel
    steps = np.arange(head // 2, dtype=np.float64) * (-2.0 * math.log(rope_base) / head)
    frequency = np.tile(np.exp(steps), 2).astype(np.float32)
    arguments = (
        positions,
        router_logits,
        queries[0],
        keys[0],
        values[0],
        out_cotangent[0],
        query_gain[None],
        key_gain[None],
        jnp.asarray(frequency)[None],
    )
    anywhere = pl.BlockSpec(memory_space=pl.ANY)
    vmem = pl.BlockSpec(memory_space=pltpu.VMEM)
    dma = pltpu.SemaphoreType.DMA
    n_g = 3 + n_seg * n_dp
    results = pl.pallas_call(
        functools.partial(kernel, n_seg, n_dp),
        out_shape=(
            jax.ShapeDtypeStruct((cap, width_q), BF16),
            jax.ShapeDtypeStruct((cap, width_q), BF16),
            jax.ShapeDtypeStruct((cap, width_k), BF16),
            jax.ShapeDtypeStruct((cap, width_k), BF16),
            jax.ShapeDtypeStruct((1, cap), F32),
            jax.ShapeDtypeStruct((1, head), F32),
            jax.ShapeDtypeStruct((1, head), F32),
        ),
        in_specs=[anywhere] * len(arguments),
        out_specs=(vmem,) * 7,
        scratch_shapes=[pltpu.VMEM(a.shape, a.dtype) for a in arguments]
        + [
            dma((len(arguments),)),
            pltpu.VMEM((SEG_DEV, pad, 2 * head), BF16),
            pltpu.VMEM((SEG_DEV, pad, 2 * head), BF16),
            pltpu.VMEM((SEG_DEV - 1, cap, gw), BF16),
            pltpu.VMEM((SEG_DEV, pad, gw), BF16),
            pltpu.VMEM((SEG_DEV - 1, cap, gw), BF16),
            pltpu.VMEM((SEG_DEV, pad, gw), BF16),
            pltpu.VMEM((heads_q, cap, head), F32),
            pltpu.VMEM((heads_q, cap, head), F32),
            pltpu.VMEM((heads_q, cap, head), BF16),
            pltpu.VMEM((heads_k, cap, head), F32),
            pltpu.VMEM((heads_k, cap, head), F32),
            pltpu.VMEM((n_seg, sel, 2 * head), BF16),
            pltpu.VMEM((n_seg, sel, 2 * head), F32),
            pltpu.VMEM((n_seg, sel, 2 * head), F32),
            pltpu.VMEM((SEG_DEV, pad, gw), BF16),
            pltpu.VMEM((SEG_DEV, cap, gw), BF16),
            pltpu.VMEM((SEG_DEV, pad, gw), BF16),
            pltpu.VMEM((SEG_DEV, cap, gw), BF16),
            pltpu.VMEM((SEG_DEV, pad, 2 * head), BF16),
            pltpu.VMEM((SEG_DEV, cap, 2 * head), BF16),
            pltpu.VMEM((SEG_DEV, 8, head), F32),
            pltpu.VMEM((n_seg * n_dp, 8, head), F32),
            dma((SEG_DEV,)),
            dma((SEG_DEV,)),
            dma((SEG_DEV,)),
            dma((SEG_DEV,)),
            dma((SEG_DEV,)),
            dma((SEG_DEV,)),
            dma((n_seg,)),
            dma((n_seg,)),
            dma((n_seg,)),
            dma((n_seg,)),
            dma((SEG_DEV,)),
            dma((SEG_DEV,)),
            dma((SEG_DEV,)),
            dma((SEG_DEV,)),
            dma((SEG_DEV,)),
            dma((SEG_DEV,)),
            dma((n_g,)),
            dma((n_g,)),
        ],
        compiler_params=pltpu.CompilerParams(
            collective_id=0, has_side_effects=True, vmem_limit_bytes=56 * 1024 * 1024
        ),
    )(*arguments)
    count = len(results)
    out, gq, gk, gv, gl, gain_q, gain_k = pl.pallas_call(
        place_results,
        out_shape=tuple(jax.ShapeDtypeStruct(r.shape, r.dtype) for r in results),
        in_specs=[anywhere] * count,
        out_specs=(anywhere,) * count,
        scratch_shapes=[pltpu.VMEM(r.shape, r.dtype) for r in results]
        + [dma((count,)), dma((count,))],
        compiler_params=pltpu.CompilerParams(vmem_limit_bytes=56 * 1024 * 1024),
    )(*results)
    return (
        out[None],
        gq[None],
        gk[None],
        gv[None],
        gl,
        gain_q.reshape(head),
        gain_k.reshape(head),
    )


def solution(mesh):
    n_seg = mesh.shape["ctx"] // SEG_DEV
    n_dp = mesh.shape["dp"]
    return jax.shard_map(
        functools.partial(per_device, n_seg, n_dp),
        mesh=mesh,
        in_specs=(
            P("dp", "ctx"),
            P("dp", "ctx", None),
            P("dp", "ctx", None),
            P("dp", "ctx", None),
            P("dp", "ctx"),
            P("dp", "ctx", None),
            P(),
            P(),
        ),
        out_specs=(
            P("dp", "ctx", None),
            P("dp", "ctx", None),
            P("dp", "ctx", None),
            P("dp", "ctx", None),
            P("dp", "ctx"),
            P(),
            P(),
        ),
        check_vma=False,
    )
```

```python
import functools
import math

import jax
import jax.numpy as jnp
import numpy as np
from jax import lax
from jax.experimental import pallas as pl
from jax.experimental.pallas import tpu as pltpu
from jax.sharding import PartitionSpec as P

SEL_DEV = 16
SEG_DEV = 4

rope_base = 1000000.0
norm_eps = 1e-06

F32 = jnp.float32
BF16 = jnp.bfloat16


def dot(a, b, dims):
    return lax.dot_general(a, b, (dims, ((), ())), preferred_element_type=F32)


NN = ((1,), (0,))
NT = ((1,), (1,))
TN = ((0,), (0,))


def kernel(
    n_seg,
    n_dp,
    pos_hbm,
    logit_hbm,
    q_hbm,
    k_hbm,
    v_hbm,
    c_hbm,
    gq_in_hbm,
    gk_in_hbm,
    freq_hbm,
    out_hbm,
    gq_hbm,
    gk_hbm,
    gv_hbm,
    gl_hbm,
    gains_q_hbm,
    gains_k_hbm,
    out_ref,
    gq_ref,
    gk_ref,
    gv_ref,
    gl_ref,
    gains_q_ref,
    gains_k_ref,
    out_s,
    pos_ref,
    logit_ref,
    q_ref,
    k_ref,
    v_ref,
    c_ref,
    gq_in_ref,
    gk_in_ref,
    freq_ref,
    in_s,
    skv,
    rkv,
    sq,
    rq,
    sd,
    rd,
    qunit,
    qinv,
    dround,
    kunit,
    kinv,
    kv_all,
    dkv_p,
    dkv_r,
    satt,
    ratt,
    sdq,
    rdq,
    skb,
    rkb,
    gplane,
    gall,
    kv_s,
    kv_r,
    q_s,
    q_r,
    d_s,
    d_r,
    z_s,
    z_r,
    dz_s,
    dz_r,
    b_s,
    b_r,
    e_s,
    e_r,
    kb_s,
    kb_r,
    g_s,
    g_r,
):
    given = (
        (pos_hbm, pos_ref),
        (logit_hbm, logit_ref),
        (freq_hbm, freq_ref),
        (gk_in_hbm, gk_in_ref),
        (k_hbm, k_ref),
        (v_hbm, v_ref),
        (gq_in_hbm, gq_in_ref),
        (q_hbm, q_ref),
        (c_hbm, c_ref),
    )
    loads = [pltpu.make_async_copy(a, b, in_s.at[i]) for i, (a, b) in enumerate(given)]
    for load in loads:
        load.start()
    made = (
        (out_ref, out_hbm),
        (gl_ref, gl_hbm),
        (gq_ref, gq_hbm),
        (gk_ref, gk_hbm),
        (gv_ref, gv_hbm),
        (gains_q_ref, gains_q_hbm),
        (gains_k_ref, gains_k_hbm),
    )
    saves = [pltpu.make_async_copy(a, b, out_s.at[i]) for i, (a, b) in enumerate(made)]
    cap, width_q = q_ref.shape
    width_k = k_ref.shape[1]
    head = freq_ref.shape[1]
    heads_k = width_k // head
    group = width_q // width_k
    gw = group * head
    sel = SEL_DEV * SEG_DEV
    pad = rkv.shape[1]
    scale = 1.0 / math.sqrt(head)

    my_dp = lax.axis_index("dp")
    my_ctx = lax.axis_index("ctx")
    seg = my_ctx // SEG_DEV
    g = my_ctx % SEG_DEV
    mate = {0: g, 1: g + 1 - 2 * (g % 2), 2: (g + 2) % 4, 3: 3 - g}
    plane = {o: seg * SEG_DEV + mate[o] for o in (1, 2, 3)}
    far = {o: (seg + o) % n_seg for o in range(1, n_seg)}
    far_dev = {o: far[o] * SEG_DEV + g for o in far}
    cells = n_dp * n_seg
    cell = my_dp * n_seg + seg
    others = {o: (cell + o) % cells for o in range(1, cells)}
    order = (2, 3, 1)

    def remote(src, dst, ssem, rsem, ctx=None, dp=None):
        return pltpu.make_async_remote_copy(
            src_ref=src,
            dst_ref=dst,
            send_sem=ssem,
            recv_sem=rsem,
            device_id=(my_dp if dp is None else dp, my_ctx if ctx is None else ctx),
            device_id_type=pl.DeviceIdType.MESH,
        )

    barrier = pltpu.get_barrier_semaphore()
    peers = [(my_dp, plane[o]) for o in order]
    peers += [(c // n_seg, c % n_seg * SEG_DEV + g) for c in others.values()]
    for peer in peers:
        pl.semaphore_signal(barrier, inc=1, device_id=peer, device_id_type=pl.DeviceIdType.MESH)

    eye = lax.broadcasted_iota(jnp.int32, (cap, cap), 0) == lax.broadcasted_iota(
        jnp.int32, (cap, cap), 1
    )

    def column(line):
        return jnp.sum(jnp.where(eye, line, 0.0), axis=1, keepdims=True)

    for load in loads[:6]:
        load.wait()
    pos = jnp.broadcast_to(column(pos_ref[...].astype(F32)), (cap, head))
    valid = jnp.where(pos >= 0.0, 1.0, 0.0)
    angle = pos * freq_ref[...]
    cos = jnp.cos(angle)
    sin = jnp.sin(angle)
    sin = jnp.where(lax.broadcasted_iota(jnp.int32, (cap, head), 1) < head // 2, -sin, sin)
    gate = jax.nn.sigmoid(jnp.broadcast_to(column(logit_ref[...]), (cap, head)))
    gain_k = gk_in_ref[...]

    def normed(x):
        inv = lax.rsqrt(jnp.mean(x * x, axis=-1, keepdims=True) + norm_eps)
        return x * inv, inv

    def rot(x, direction):
        turned = pltpu.roll(x, head // 2, axis=1) * sin
        return x * cos + turned if direction > 0 else x * cos - turned

    count = jnp.sum(valid, axis=0, keepdims=True)
    count = jnp.broadcast_to(jnp.concatenate([count, count], axis=1), (pad - cap, 2 * head))
    for t in range(heads_k):
        cols = pl.ds(t * head, head)
        unit, inv = normed(k_ref[:, cols].astype(F32))
        kunit[t] = unit
        kinv[t] = jnp.broadcast_to(inv, (cap, head))
        skv[t, 0:cap, 0:head] = rot(unit * gain_k, 1).astype(BF16)
        skv[t, 0:cap, head:] = v_ref[:, cols]
        skv[t, cap:, :] = count.astype(BF16)

    pl.semaphore_wait(barrier, len(peers))

    kv_copies = []
    for o in order:
        copy = remote(skv.at[mate[o]], rkv.at[g], kv_s.at[o], kv_r.at[o], ctx=plane[o])
        copy.start()
        kv_copies.append(copy)
    rkv[g] = skv[g]

    q_copies = []
    d_copies = []
    for load in loads[6:8]:
        load.wait()
    gain_q = gq_in_ref[...]
    for o in order + (0,):
        t = mate[o]
        for j in range(group):
            cols = pl.ds(pl.multiple_of(t * gw + j * head, head), head)
            unit, inv = normed(q_ref[:, cols].astype(F32))
            qunit[t * group + j] = unit
            qinv[t * group + j] = jnp.broadcast_to(inv, (cap, head))
            turned = rot(unit * gain_q, 1).astype(BF16)
            if o == 0:
                rq[g, 0:cap, j * head : (j + 1) * head] = turned
            else:
                sq[o - 1, :, j * head : (j + 1) * head] = turned
        if o != 0:
            copy = remote(
                sq.at[o - 1], rq.at[g, pl.ds(0, cap)], q_s.at[o], q_r.at[o], ctx=plane[o]
            )
            copy.start()
            q_copies.append(copy)
    loads[8].wait()
    for o in order + (0,):
        t = mate[o]
        for j in range(group):
            cols = pl.ds(pl.multiple_of(t * gw + j * head, head), head)
            weighted = (gate * c_ref[:, cols].astype(F32)).astype(BF16)
            dround[t * group + j] = weighted
            if o == 0:
                rd[g, 0:cap, j * head : (j + 1) * head] = weighted
            else:
                sd[o - 1, :, j * head : (j + 1) * head] = weighted
        if o != 0:
            copy = remote(
                sd.at[o - 1], rd.at[g, pl.ds(0, cap)], d_s.at[o], d_r.at[o], ctx=plane[o]
            )
            copy.start()
            d_copies.append(copy)
    for m in range(SEG_DEV):
        rq[m, cap:, :] = jnp.zeros((pad - cap, gw), BF16)
        rd[m, cap:, :] = jnp.zeros((pad - cap, gw), BF16)

    for copy in kv_copies:
        copy.wait_recv()
    wide = SEG_DEV * pad
    lane = lax.broadcasted_iota(jnp.int32, (1, wide), 1)
    member = lane // pad
    slot = (lane % pad).astype(F32)
    counts = [rkv[m, cap : cap + 16, :].astype(F32)[0:1] for m in range(SEG_DEV)]
    have = counts[0]
    base = jnp.zeros_like(have)
    run = counts[0]
    for m in range(1, SEG_DEV):
        have = jnp.where(member == m, counts[m], have)
        base = jnp.where(member == m, run, base)
        run = run + counts[m]
    place = jnp.where(slot < have, base + slot, -1.0)
    rank = lax.broadcasted_iota(jnp.int32, (sel, wide), 0).astype(F32)
    pick = jnp.where(rank == place, 1.0, 0.0).astype(BF16)
    kv_all[seg] = dot(pick, rkv[...].reshape(wide, 2 * head), NN).astype(BF16)
    z_copies = []
    for o in far:
        copy = remote(kv_all.at[seg], kv_all.at[seg], z_s.at[o], z_r.at[o], ctx=far_dev[o])
        copy.start()
        z_copies.append(copy)

    def heads_down(wide_rows):
        return jnp.concatenate(
            [wide_rows[:, j * head : (j + 1) * head] for j in range(group)], axis=0
        )

    def heads_across(tall_rows):
        return jnp.concatenate([tall_rows[j * sel : (j + 1) * sel] for j in range(group)], axis=1)

    for copy in q_copies:
        copy.wait_recv()
    q_rows = heads_down(dot(pick, rq[...].reshape(wide, gw), NN).astype(BF16))
    for copy in z_copies:
        copy.wait_recv()

    total = n_seg * sel
    keys = kv_all[:, :, 0:head].reshape(total, head)
    vals = kv_all[:, :, head:].reshape(total, head)
    row = lax.broadcasted_iota(jnp.int32, (group * sel, total), 0) % sel
    col = lax.broadcasted_iota(jnp.int32, (group * sel, total), 1)
    scores = dot(q_rows, keys, NT) * scale
    scores = jnp.where(col <= row + seg * sel, scores, -jnp.inf)
    top = jnp.max(scores, axis=-1, keepdims=True)
    exps = jnp.exp(scores - top)
    probs = exps / jnp.sum(exps, axis=-1, keepdims=True)
    probs_b = probs.astype(BF16)
    attended = dot(probs_b, vals, NN).astype(BF16)
    satt[...] = dot(pick, heads_across(attended), TN).astype(BF16).reshape(SEG_DEV, pad, gw)
    b_copies = []
    for o in order:
        copy = remote(
            satt.at[mate[o], pl.ds(0, cap)], ratt.at[g], b_s.at[o], b_r.at[o], ctx=plane[o]
        )
        copy.start()
        b_copies.append(copy)
    ratt[g] = satt[g, 0:cap]

    for copy in d_copies:
        copy.wait_recv()
    d_rows = heads_down(dot(pick, rd[...].reshape(wide, gw), NN).astype(BF16))
    delta = jnp.sum(d_rows.astype(F32) * attended.astype(F32), axis=-1, keepdims=True)
    dprob = dot(d_rows, vals, NT)
    dscore = (probs * (dprob - delta)).astype(BF16)
    dkv_p[:, :, 0:head] = (dot(dscore, q_rows, TN) * scale).reshape(n_seg, sel, head)
    dkv_p[:, :, head:] = dot(probs_b, d_rows, TN).reshape(n_seg, sel, head)
    dz_copies = []
    for o in far:
        copy = remote(dkv_p.at[far[o]], dkv_r.at[seg], dz_s.at[o], dz_r.at[o], ctx=far_dev[o])
        copy.start()
        dz_copies.append(copy)
    dkv_r[seg] = dkv_p[seg]

    dq = (dot(dscore, keys, NN) * scale).astype(BF16)
    sdq[...] = dot(pick, heads_across(dq), TN).astype(BF16).reshape(SEG_DEV, pad, gw)
    e_copies = []
    for o in order:
        copy = remote(
            sdq.at[mate[o], pl.ds(0, cap)], rdq.at[g], e_s.at[o], e_r.at[o], ctx=plane[o]
        )
        copy.start()
        e_copies.append(copy)
    rdq[g] = sdq[g, 0:cap]

    logit = jnp.zeros((cap, head), F32)
    for copy in b_copies:
        copy.wait_recv()
    for t in range(SEG_DEV):
        for j in range(group):
            cols = pl.ds(t * gw + j * head, head)
            att = ratt[t, :, j * head : (j + 1) * head].astype(F32)
            out_ref[:, cols] = (gate * att).astype(BF16)
            logit = logit + dround[t * group + j].astype(F32) * att
    total_logit = (1.0 - gate[:, 0:1]) * jnp.sum(logit, axis=-1, keepdims=True)
    gl_ref[...] = jnp.sum(jnp.where(eye, total_logit, 0.0), axis=0, keepdims=True)

    saves[0].start()
    saves[1].start()

    def norm_back(grad, unit, inv, gain):
        turned = rot(grad.astype(F32), -1)
        term = jnp.sum(turned * unit, axis=0, keepdims=True)
        scaled = turned * gain
        mean = jnp.mean(scaled * unit, axis=-1, keepdims=True)
        return (inv * (scaled - unit * mean)).astype(BF16), term

    def query_back(o, term_q):
        t = mate[o]
        for j in range(group):
            cols = pl.ds(pl.multiple_of(t * gw + j * head, head), head)
            grad, term = norm_back(
                rdq[t, :, j * head : (j + 1) * head],
                qunit[t * group + j],
                qinv[t * group + j],
                gain_q,
            )
            gq_ref[:, cols] = grad
            term_q = term_q + term
        return term_q

    term_q = query_back(0, jnp.zeros((1, head), F32))

    for copy in dz_copies:
        copy.wait_recv()
    dkv = dkv_r[0]
    for s in range(1, n_seg):
        dkv = dkv + dkv_r[s]
    skb[...] = dot(pick, dkv.astype(BF16), TN).astype(BF16).reshape(SEG_DEV, pad, 2 * head)
    kb_copies = []
    for o in order:
        copy = remote(
            skb.at[mate[o], pl.ds(0, cap)], rkb.at[g], kb_s.at[o], kb_r.at[o], ctx=plane[o]
        )
        copy.start()
        kb_copies.append(copy)
    rkb[g] = skb[g, 0:cap]

    for o, copy in zip((1, 2, 3), (e_copies[2], e_copies[0], e_copies[1])):
        copy.wait_recv()
        term_q = query_back(o, term_q)

    saves[2].start()
    for copy in kb_copies:
        copy.wait_recv()
    term_k = jnp.zeros((1, head), F32)
    for t in range(heads_k):
        cols = pl.ds(t * head, head)
        grad, term = norm_back(rkb[t, :, 0:head], kunit[t], kinv[t], gain_k)
        gk_ref[:, cols] = grad
        gv_ref[:, cols] = rkb[t, :, head:]
        term_k = term_k + term

    saves[3].start()
    saves[4].start()

    which = lax.broadcasted_iota(jnp.int32, (8, head), 0)
    terms = jnp.where(which == 0, term_q, jnp.where(which == 1, term_k, 0.0))
    last = []
    gplane[g] = terms
    stage = []
    for o in order:
        copy = remote(gplane.at[g], gplane.at[g], g_s.at[o], g_r.at[o], ctx=plane[o])
        copy.start()
        stage.append(copy)
    for copy in stage:
        copy.wait_recv()
    last += stage
    terms = gplane[0] + gplane[1] + gplane[2] + gplane[3]
    gall[cell] = terms
    stage = []
    for o, c in others.items():
        copy = remote(
            gall.at[cell],
            gall.at[cell],
            g_s.at[3 + o],
            g_r.at[3 + o],
            ctx=c % n_seg * SEG_DEV + g,
            dp=c // n_seg,
        )
        copy.start()
        stage.append(copy)
    for copy in stage:
        copy.wait_recv()
    last += stage
    terms = gall[0]
    for s in range(1, cells):
        terms = terms + gall[s]
    selected_all = n_dp * total
    over_q = 1.0 / math.sqrt(selected_all * group * heads_k)
    over_k = 1.0 / math.sqrt(selected_all * heads_k)
    gains_q_ref[...] = terms[0:1] * over_q
    gains_k_ref[...] = terms[1:2] * over_k

    saves[5].start()
    saves[6].start()
    for save in saves:
        save.wait()
    mine = kv_copies + q_copies + d_copies + z_copies + dz_copies
    for copy in mine + b_copies + e_copies + kb_copies + last:
        copy.wait_send()


def place_results(*refs):
    count = (len(refs) - 2) // 3
    given, placed, held = (refs[i * count : (i + 1) * count] for i in range(3))
    load_s, store_s = refs[-2:]
    loads = [pltpu.make_async_copy(given[i], held[i], load_s.at[i]) for i in range(count)]
    stores = [pltpu.make_async_copy(held[i], placed[i], store_s.at[i]) for i in range(count)]
    for load in loads:
        load.start()
    for load, store in zip(loads, stores):
        load.wait()
        store.start()
    for store in stores:
        store.wait()


def per_device(
    n_seg,
    n_dp,
    positions,
    queries,
    keys,
    values,
    router_logits,
    out_cotangent,
    query_gain,
    key_gain,
):
    cap = positions.shape[1]
    head = query_gain.shape[0]
    width_q = queries.shape[2]
    width_k = keys.shape[2]
    heads_q = width_q // head
    heads_k = width_k // head
    gw = width_q // heads_k
    sel = SEL_DEV * SEG_DEV
    pad = sel
    steps = np.arange(head // 2, dtype=np.float64) * (-2.0 * math.log(rope_base) / head)
    frequency = np.tile(np.exp(steps), 2).astype(np.float32)
    arguments = (
        positions,
        router_logits,
        queries[0],
        keys[0],
        values[0],
        out_cotangent[0],
        query_gain[None],
        key_gain[None],
        jnp.asarray(frequency)[None],
    )
    anywhere = pl.BlockSpec(memory_space=pl.ANY)
    dma = pltpu.SemaphoreType.DMA
    n_g = 3 + n_seg * n_dp
    made = (
            jax.ShapeDtypeStruct((cap, width_q), BF16),
            jax.ShapeDtypeStruct((cap, width_q), BF16),
            jax.ShapeDtypeStruct((cap, width_k), BF16),
            jax.ShapeDtypeStruct((cap, width_k), BF16),
            jax.ShapeDtypeStruct((1, cap), F32),
            jax.ShapeDtypeStruct((1, head), F32),
            jax.ShapeDtypeStruct((1, head), F32),
        )
    results = pl.pallas_call(
        functools.partial(kernel, n_seg, n_dp),
        out_shape=made,
        in_specs=[anywhere] * len(arguments),
        out_specs=(anywhere,) * len(made),
        scratch_shapes=[pltpu.VMEM(a.shape, a.dtype) for a in made]
        + [dma((len(made),))]
        + [pltpu.VMEM(a.shape, a.dtype) for a in arguments]
        + [
            dma((len(arguments),)),
            pltpu.VMEM((SEG_DEV, pad, 2 * head), BF16),
            pltpu.VMEM((SEG_DEV, pad, 2 * head), BF16),
            pltpu.VMEM((SEG_DEV - 1, cap, gw), BF16),
            pltpu.VMEM((SEG_DEV, pad, gw), BF16),
            pltpu.VMEM((SEG_DEV - 1, cap, gw), BF16),
            pltpu.VMEM((SEG_DEV, pad, gw), BF16),
            pltpu.VMEM((heads_q, cap, head), F32),
            pltpu.VMEM((heads_q, cap, head), F32),
            pltpu.VMEM((heads_q, cap, head), BF16),
            pltpu.VMEM((heads_k, cap, head), F32),
            pltpu.VMEM((heads_k, cap, head), F32),
            pltpu.VMEM((n_seg, sel, 2 * head), BF16),
            pltpu.VMEM((n_seg, sel, 2 * head), F32),
            pltpu.VMEM((n_seg, sel, 2 * head), F32),
            pltpu.VMEM((SEG_DEV, pad, gw), BF16),
            pltpu.VMEM((SEG_DEV, cap, gw), BF16),
            pltpu.VMEM((SEG_DEV, pad, gw), BF16),
            pltpu.VMEM((SEG_DEV, cap, gw), BF16),
            pltpu.VMEM((SEG_DEV, pad, 2 * head), BF16),
            pltpu.VMEM((SEG_DEV, cap, 2 * head), BF16),
            pltpu.VMEM((SEG_DEV, 8, head), F32),
            pltpu.VMEM((n_seg * n_dp, 8, head), F32),
            dma((SEG_DEV,)),
            dma((SEG_DEV,)),
            dma((SEG_DEV,)),
            dma((SEG_DEV,)),
            dma((SEG_DEV,)),
            dma((SEG_DEV,)),
            dma((n_seg,)),
            dma((n_seg,)),
            dma((n_seg,)),
            dma((n_seg,)),
            dma((SEG_DEV,)),
            dma((SEG_DEV,)),
            dma((SEG_DEV,)),
            dma((SEG_DEV,)),
            dma((SEG_DEV,)),
            dma((SEG_DEV,)),
            dma((n_g,)),
            dma((n_g,)),
        ],
        compiler_params=pltpu.CompilerParams(
            collective_id=0, has_side_effects=True, vmem_limit_bytes=56 * 1024 * 1024
        ),
    )(*arguments)
    count = len(results)
    out, gq, gk, gv, gl, gain_q, gain_k = pl.pallas_call(
        place_results,
        out_shape=tuple(jax.ShapeDtypeStruct(r.shape, r.dtype) for r in results),
        in_specs=[anywhere] * count,
        out_specs=(anywhere,) * count,
        scratch_shapes=[pltpu.VMEM(r.shape, r.dtype) for r in results]
        + [dma((count,)), dma((count,))],
        compiler_params=pltpu.CompilerParams(vmem_limit_bytes=56 * 1024 * 1024),
    )(*results)
    return (
        out[None],
        gq[None],
        gk[None],
        gv[None],
        gl,
        gain_q.reshape(head),
        gain_k.reshape(head),
    )


def solution(mesh):
    n_seg = mesh.shape["ctx"] // SEG_DEV
    n_dp = mesh.shape["dp"]
    return jax.shard_map(
        functools.partial(per_device, n_seg, n_dp),
        mesh=mesh,
        in_specs=(
            P("dp", "ctx"),
            P("dp", "ctx", None),
            P("dp", "ctx", None),
            P("dp", "ctx", None),
            P("dp", "ctx"),
            P("dp", "ctx", None),
            P(),
            P(),
        ),
        out_specs=(
            P("dp", "ctx", None),
            P("dp", "ctx", None),
            P("dp", "ctx", None),
            P("dp", "ctx", None),
            P("dp", "ctx"),
            P(),
            P(),
        ),
        check_vma=False,
    )
```

```python
import functools
import math

import jax
import jax.numpy as jnp
import numpy as np
from jax import lax
from jax.experimental import pallas as pl
from jax.experimental.pallas import tpu as pltpu
from jax.sharding import PartitionSpec as P

SEL_DEV = 16
SEG_DEV = 4

rope_base = 1000000.0
norm_eps = 1e-06

F32 = jnp.float32
BF16 = jnp.bfloat16


def dot(a, b, dims):
    return lax.dot_general(a, b, (dims, ((), ())), preferred_element_type=F32)


NN = ((1,), (0,))
NT = ((1,), (1,))
TN = ((0,), (0,))


def kernel(
    n_seg,
    n_dp,
    pos_hbm,
    logit_hbm,
    q_hbm,
    k_hbm,
    v_hbm,
    c_hbm,
    gq_in_hbm,
    gk_in_hbm,
    freq_hbm,
    out_hbm,
    gq_hbm,
    gk_hbm,
    gv_hbm,
    gl_hbm,
    gains_q_hbm,
    gains_k_hbm,
    out_ref,
    gq_ref,
    gk_ref,
    gv_ref,
    gl_ref,
    gains_q_ref,
    gains_k_ref,
    out_s,
    pos_ref,
    logit_ref,
    q_ref,
    k_ref,
    v_ref,
    c_ref,
    gq_in_ref,
    gk_in_ref,
    freq_ref,
    in_s,
    skv,
    rkv,
    sq,
    rq,
    sd,
    rd,
    qunit,
    qinv,
    dround,
    kunit,
    kinv,
    kv_all,
    dkv_p,
    dkv_h,
    dkv_r,
    satt,
    ratt,
    sdq,
    rdq,
    skb,
    rkb,
    gplane,
    gall,
    kv_s,
    kv_r,
    q_s,
    q_r,
    d_s,
    d_r,
    z_s,
    z_r,
    dz_s,
    dz_r,
    b_s,
    b_r,
    e_s,
    e_r,
    kb_s,
    kb_r,
    g_s,
    g_r,
):
    given = (
        (pos_hbm, pos_ref),
        (logit_hbm, logit_ref),
        (freq_hbm, freq_ref),
        (gk_in_hbm, gk_in_ref),
        (k_hbm, k_ref),
        (v_hbm, v_ref),
        (gq_in_hbm, gq_in_ref),
        (q_hbm, q_ref),
        (c_hbm, c_ref),
    )
    loads = [pltpu.make_async_copy(a, b, in_s.at[i]) for i, (a, b) in enumerate(given)]
    for load in loads:
        load.start()
    made = (
        (out_ref, out_hbm),
        (gl_ref, gl_hbm),
        (gq_ref, gq_hbm),
        (gk_ref, gk_hbm),
        (gv_ref, gv_hbm),
        (gains_q_ref, gains_q_hbm),
        (gains_k_ref, gains_k_hbm),
    )
    saves = [pltpu.make_async_copy(a, b, out_s.at[i]) for i, (a, b) in enumerate(made)]
    cap, width_q = q_ref.shape
    width_k = k_ref.shape[1]
    head = freq_ref.shape[1]
    heads_k = width_k // head
    group = width_q // width_k
    gw = group * head
    sel = SEL_DEV * SEG_DEV
    pad = rkv.shape[1]
    scale = 1.0 / math.sqrt(head)

    my_dp = lax.axis_index("dp")
    my_ctx = lax.axis_index("ctx")
    seg = my_ctx // SEG_DEV
    g = my_ctx % SEG_DEV
    mate = {0: g, 1: g + 1 - 2 * (g % 2), 2: (g + 2) % 4, 3: 3 - g}
    plane = {o: seg * SEG_DEV + mate[o] for o in (1, 2, 3)}
    far = {o: (seg + o) % n_seg for o in range(1, n_seg)}
    far_dev = {o: far[o] * SEG_DEV + g for o in far}
    cells = n_dp * n_seg
    cell = my_dp * n_seg + seg
    others = {o: (cell + o) % cells for o in range(1, cells)}
    order = (2, 3, 1)

    def remote(src, dst, ssem, rsem, ctx=None, dp=None):
        return pltpu.make_async_remote_copy(
            src_ref=src,
            dst_ref=dst,
            send_sem=ssem,
            recv_sem=rsem,
            device_id=(my_dp if dp is None else dp, my_ctx if ctx is None else ctx),
            device_id_type=pl.DeviceIdType.MESH,
        )

    barrier = pltpu.get_barrier_semaphore()
    peers = [(my_dp, plane[o]) for o in order]
    peers += [(c // n_seg, c % n_seg * SEG_DEV + g) for c in others.values()]
    for peer in peers:
        pl.semaphore_signal(barrier, inc=1, device_id=peer, device_id_type=pl.DeviceIdType.MESH)

    eye = lax.broadcasted_iota(jnp.int32, (cap, cap), 0) == lax.broadcasted_iota(
        jnp.int32, (cap, cap), 1
    )

    def column(line):
        return jnp.sum(jnp.where(eye, line, 0.0), axis=1, keepdims=True)

    for load in loads[:6]:
        load.wait()
    pos = jnp.broadcast_to(column(pos_ref[...].astype(F32)), (cap, head))
    valid = jnp.where(pos >= 0.0, 1.0, 0.0)
    angle = pos * freq_ref[...]
    cos = jnp.cos(angle)
    sin = jnp.sin(angle)
    sin = jnp.where(lax.broadcasted_iota(jnp.int32, (cap, head), 1) < head // 2, -sin, sin)
    gate = jax.nn.sigmoid(jnp.broadcast_to(column(logit_ref[...]), (cap, head)))
    gain_k = gk_in_ref[...]

    def normed(x):
        inv = lax.rsqrt(jnp.mean(x * x, axis=-1, keepdims=True) + norm_eps)
        return x * inv, inv

    def rot(x, direction):
        turned = pltpu.roll(x, head // 2, axis=1) * sin
        return x * cos + turned if direction > 0 else x * cos - turned

    count = jnp.sum(valid, axis=0, keepdims=True)
    count = jnp.broadcast_to(jnp.concatenate([count, count], axis=1), (pad - cap, 2 * head))
    for t in range(heads_k):
        cols = pl.ds(t * head, head)
        unit, inv = normed(k_ref[:, cols].astype(F32))
        kunit[t] = unit
        kinv[t] = jnp.broadcast_to(inv, (cap, head))
        skv[t, 0:cap, 0:head] = rot(unit * gain_k, 1).astype(BF16)
        skv[t, 0:cap, head:] = v_ref[:, cols]
        skv[t, cap:, :] = count.astype(BF16)

    pl.semaphore_wait(barrier, len(peers))

    kv_copies = []
    for o in order:
        copy = remote(skv.at[mate[o]], rkv.at[g], kv_s.at[o], kv_r.at[o], ctx=plane[o])
        copy.start()
        kv_copies.append(copy)
    rkv[g] = skv[g]

    q_copies = []
    d_copies = []
    for load in loads[6:8]:
        load.wait()
    gain_q = gq_in_ref[...]
    for o in order + (0,):
        t = mate[o]
        for j in range(group):
            cols = pl.ds(pl.multiple_of(t * gw + j * head, head), head)
            unit, inv = normed(q_ref[:, cols].astype(F32))
            qunit[t * group + j] = unit
            qinv[t * group + j] = jnp.broadcast_to(inv, (cap, head))
            turned = rot(unit * gain_q, 1).astype(BF16)
            if o == 0:
                rq[g, 0:cap, j * head : (j + 1) * head] = turned
            else:
                sq[o - 1, :, j * head : (j + 1) * head] = turned
        if o != 0:
            copy = remote(
                sq.at[o - 1], rq.at[g, pl.ds(0, cap)], q_s.at[o], q_r.at[o], ctx=plane[o]
            )
            copy.start()
            q_copies.append(copy)
    loads[8].wait()
    for o in order + (0,):
        t = mate[o]
        for j in range(group):
            cols = pl.ds(pl.multiple_of(t * gw + j * head, head), head)
            weighted = (gate * c_ref[:, cols].astype(F32)).astype(BF16)
            dround[t * group + j] = weighted
            if o == 0:
                rd[g, 0:cap, j * head : (j + 1) * head] = weighted
            else:
                sd[o - 1, :, j * head : (j + 1) * head] = weighted
        if o != 0:
            copy = remote(
                sd.at[o - 1], rd.at[g, pl.ds(0, cap)], d_s.at[o], d_r.at[o], ctx=plane[o]
            )
            copy.start()
            d_copies.append(copy)
    for m in range(SEG_DEV):
        rq[m, cap:, :] = jnp.zeros((pad - cap, gw), BF16)
        rd[m, cap:, :] = jnp.zeros((pad - cap, gw), BF16)

    for copy in kv_copies:
        copy.wait_recv()
    wide = SEG_DEV * pad
    lane = lax.broadcasted_iota(jnp.int32, (1, wide), 1)
    member = lane // pad
    slot = (lane % pad).astype(F32)
    counts = [rkv[m, cap : cap + 16, :].astype(F32)[0:1] for m in range(SEG_DEV)]
    have = counts[0]
    base = jnp.zeros_like(have)
    run = counts[0]
    for m in range(1, SEG_DEV):
        have = jnp.where(member == m, counts[m], have)
        base = jnp.where(member == m, run, base)
        run = run + counts[m]
    place = jnp.where(slot < have, base + slot, -1.0)
    rank = lax.broadcasted_iota(jnp.int32, (sel, wide), 0).astype(F32)
    pick = jnp.where(rank == place, 1.0, 0.0).astype(BF16)
    kv_all[seg] = dot(pick, rkv[...].reshape(wide, 2 * head), NN).astype(BF16)
    z_copies = []
    for o in far:
        copy = remote(kv_all.at[seg], kv_all.at[seg], z_s.at[o], z_r.at[o], ctx=far_dev[o])
        copy.start()
        z_copies.append(copy)

    def heads_down(wide_rows):
        return jnp.concatenate(
            [wide_rows[:, j * head : (j + 1) * head] for j in range(group)], axis=0
        )

    def heads_across(tall_rows):
        return jnp.concatenate([tall_rows[j * sel : (j + 1) * sel] for j in range(group)], axis=1)

    for copy in q_copies:
        copy.wait_recv()
    q_rows = heads_down(dot(pick, rq[...].reshape(wide, gw), NN).astype(BF16))
    for copy in z_copies:
        copy.wait_recv()

    total = n_seg * sel
    keys = kv_all[:, :, 0:head].reshape(total, head)
    vals = kv_all[:, :, head:].reshape(total, head)
    row = lax.broadcasted_iota(jnp.int32, (group * sel, total), 0) % sel
    col = lax.broadcasted_iota(jnp.int32, (group * sel, total), 1)
    scores = dot(q_rows, keys, NT) * scale
    scores = jnp.where(col <= row + seg * sel, scores, -jnp.inf)
    top = jnp.max(scores, axis=-1, keepdims=True)
    exps = jnp.exp(scores - top)
    probs = exps / jnp.sum(exps, axis=-1, keepdims=True)
    probs_b = probs.astype(BF16)
    attended = dot(probs_b, vals, NN).astype(BF16)
    satt[...] = dot(pick, heads_across(attended), TN).astype(BF16).reshape(SEG_DEV, pad, gw)
    b_copies = []
    for o in order:
        copy = remote(
            satt.at[mate[o], pl.ds(0, cap)], ratt.at[g], b_s.at[o], b_r.at[o], ctx=plane[o]
        )
        copy.start()
        b_copies.append(copy)
    ratt[g] = satt[g, 0:cap]

    for copy in d_copies:
        copy.wait_recv()
    d_rows = heads_down(dot(pick, rd[...].reshape(wide, gw), NN).astype(BF16))
    delta = jnp.sum(d_rows.astype(F32) * attended.astype(F32), axis=-1, keepdims=True)
    dprob = dot(d_rows, vals, NT)
    dscore = (probs * (dprob - delta)).astype(BF16)
    dkv_p[:, :, 0:head] = (dot(dscore, q_rows, TN) * scale).reshape(n_seg, sel, head)
    dkv_p[:, :, head:] = dot(probs_b, d_rows, TN).reshape(n_seg, sel, head)
    dkv_h[...] = dkv_p[...].astype(BF16)
    dz_copies = []
    for o in far:
        copy = remote(dkv_h.at[far[o]], dkv_r.at[seg], dz_s.at[o], dz_r.at[o], ctx=far_dev[o])
        copy.start()
        dz_copies.append(copy)
    dkv_r[seg] = jnp.zeros((sel, 2 * head), BF16)

    dq = (dot(dscore, keys, NN) * scale).astype(BF16)
    sdq[...] = dot(pick, heads_across(dq), TN).astype(BF16).reshape(SEG_DEV, pad, gw)
    e_copies = []
    for o in order:
        copy = remote(
            sdq.at[mate[o], pl.ds(0, cap)], rdq.at[g], e_s.at[o], e_r.at[o], ctx=plane[o]
        )
        copy.start()
        e_copies.append(copy)
    rdq[g] = sdq[g, 0:cap]

    logit = jnp.zeros((cap, head), F32)
    for copy in b_copies:
        copy.wait_recv()
    for t in range(SEG_DEV):
        for j in range(group):
            cols = pl.ds(t * gw + j * head, head)
            att = ratt[t, :, j * head : (j + 1) * head].astype(F32)
            out_ref[:, cols] = (gate * att).astype(BF16)
            logit = logit + dround[t * group + j].astype(F32) * att
    total_logit = (1.0 - gate[:, 0:1]) * jnp.sum(logit, axis=-1, keepdims=True)
    gl_ref[...] = jnp.sum(jnp.where(eye, total_logit, 0.0), axis=0, keepdims=True)

    saves[0].start()
    saves[1].start()

    def norm_back(grad, unit, inv, gain):
        turned = rot(grad.astype(F32), -1)
        term = jnp.sum(turned * unit, axis=0, keepdims=True)
        scaled = turned * gain
        mean = jnp.mean(scaled * unit, axis=-1, keepdims=True)
        return (inv * (scaled - unit * mean)).astype(BF16), term

    def query_back(o, term_q):
        t = mate[o]
        for j in range(group):
            cols = pl.ds(pl.multiple_of(t * gw + j * head, head), head)
            grad, term = norm_back(
                rdq[t, :, j * head : (j + 1) * head],
                qunit[t * group + j],
                qinv[t * group + j],
                gain_q,
            )
            gq_ref[:, cols] = grad
            term_q = term_q + term
        return term_q

    term_q = query_back(0, jnp.zeros((1, head), F32))

    for copy in dz_copies:
        copy.wait_recv()
    dkv = dkv_p[seg]
    for s in range(n_seg):
        dkv = dkv + dkv_r[s].astype(F32)
    skb[...] = dot(pick, dkv.astype(BF16), TN).astype(BF16).reshape(SEG_DEV, pad, 2 * head)
    kb_copies = []
    for o in order:
        copy = remote(
            skb.at[mate[o], pl.ds(0, cap)], rkb.at[g], kb_s.at[o], kb_r.at[o], ctx=plane[o]
        )
        copy.start()
        kb_copies.append(copy)
    rkb[g] = skb[g, 0:cap]

    for o, copy in zip((1, 2, 3), (e_copies[2], e_copies[0], e_copies[1])):
        copy.wait_recv()
        term_q = query_back(o, term_q)

    saves[2].start()
    for copy in kb_copies:
        copy.wait_recv()
    term_k = jnp.zeros((1, head), F32)
    for t in range(heads_k):
        cols = pl.ds(t * head, head)
        grad, term = norm_back(rkb[t, :, 0:head], kunit[t], kinv[t], gain_k)
        gk_ref[:, cols] = grad
        gv_ref[:, cols] = rkb[t, :, head:]
        term_k = term_k + term

    saves[3].start()
    saves[4].start()

    which = lax.broadcasted_iota(jnp.int32, (8, head), 0)
    terms = jnp.where(which == 0, term_q, jnp.where(which == 1, term_k, 0.0))
    last = []
    gplane[g] = terms
    stage = []
    for o in order:
        copy = remote(gplane.at[g], gplane.at[g], g_s.at[o], g_r.at[o], ctx=plane[o])
        copy.start()
        stage.append(copy)
    for copy in stage:
        copy.wait_recv()
    last += stage
    terms = gplane[0] + gplane[1] + gplane[2] + gplane[3]
    gall[cell] = terms
    stage = []
    for o, c in others.items():
        copy = remote(
            gall.at[cell],
            gall.at[cell],
            g_s.at[3 + o],
            g_r.at[3 + o],
            ctx=c % n_seg * SEG_DEV + g,
            dp=c // n_seg,
        )
        copy.start()
        stage.append(copy)
    for copy in stage:
        copy.wait_recv()
    last += stage
    terms = gall[0]
    for s in range(1, cells):
        terms = terms + gall[s]
    selected_all = n_dp * total
    over_q = 1.0 / math.sqrt(selected_all * group * heads_k)
    over_k = 1.0 / math.sqrt(selected_all * heads_k)
    gains_q_ref[...] = terms[0:1] * over_q
    gains_k_ref[...] = terms[1:2] * over_k

    saves[5].start()
    saves[6].start()
    for save in saves:
        save.wait()
    mine = kv_copies + q_copies + d_copies + z_copies + dz_copies
    for copy in mine + b_copies + e_copies + kb_copies + last:
        copy.wait_send()


def place_results(*refs):
    count = (len(refs) - 2) // 3
    given, placed, held = (refs[i * count : (i + 1) * count] for i in range(3))
    load_s, store_s = refs[-2:]
    loads = [pltpu.make_async_copy(given[i], held[i], load_s.at[i]) for i in range(count)]
    stores = [pltpu.make_async_copy(held[i], placed[i], store_s.at[i]) for i in range(count)]
    for load in loads:
        load.start()
    for load, store in zip(loads, stores):
        load.wait()
        store.start()
    for store in stores:
        store.wait()


def per_device(
    n_seg,
    n_dp,
    positions,
    queries,
    keys,
    values,
    router_logits,
    out_cotangent,
    query_gain,
    key_gain,
):
    cap = positions.shape[1]
    head = query_gain.shape[0]
    width_q = queries.shape[2]
    width_k = keys.shape[2]
    heads_q = width_q // head
    heads_k = width_k // head
    gw = width_q // heads_k
    sel = SEL_DEV * SEG_DEV
    pad = sel
    steps = np.arange(head // 2, dtype=np.float64) * (-2.0 * math.log(rope_base) / head)
    frequency = np.tile(np.exp(steps), 2).astype(np.float32)
    arguments = (
        positions,
        router_logits,
        queries[0],
        keys[0],
        values[0],
        out_cotangent[0],
        query_gain[None],
        key_gain[None],
        jnp.asarray(frequency)[None],
    )
    anywhere = pl.BlockSpec(memory_space=pl.ANY)
    dma = pltpu.SemaphoreType.DMA
    n_g = 3 + n_seg * n_dp
    made = (
            jax.ShapeDtypeStruct((cap, width_q), BF16),
            jax.ShapeDtypeStruct((cap, width_q), BF16),
            jax.ShapeDtypeStruct((cap, width_k), BF16),
            jax.ShapeDtypeStruct((cap, width_k), BF16),
            jax.ShapeDtypeStruct((1, cap), F32),
            jax.ShapeDtypeStruct((1, head), F32),
            jax.ShapeDtypeStruct((1, head), F32),
        )
    results = pl.pallas_call(
        functools.partial(kernel, n_seg, n_dp),
        out_shape=made,
        in_specs=[anywhere] * len(arguments),
        out_specs=(anywhere,) * len(made),
        scratch_shapes=[pltpu.VMEM(a.shape, a.dtype) for a in made]
        + [dma((len(made),))]
        + [pltpu.VMEM(a.shape, a.dtype) for a in arguments]
        + [
            dma((len(arguments),)),
            pltpu.VMEM((SEG_DEV, pad, 2 * head), BF16),
            pltpu.VMEM((SEG_DEV, pad, 2 * head), BF16),
            pltpu.VMEM((SEG_DEV - 1, cap, gw), BF16),
            pltpu.VMEM((SEG_DEV, pad, gw), BF16),
            pltpu.VMEM((SEG_DEV - 1, cap, gw), BF16),
            pltpu.VMEM((SEG_DEV, pad, gw), BF16),
            pltpu.VMEM((heads_q, cap, head), F32),
            pltpu.VMEM((heads_q, cap, head), F32),
            pltpu.VMEM((heads_q, cap, head), BF16),
            pltpu.VMEM((heads_k, cap, head), F32),
            pltpu.VMEM((heads_k, cap, head), F32),
            pltpu.VMEM((n_seg, sel, 2 * head), BF16),
            pltpu.VMEM((n_seg, sel, 2 * head), F32),
            pltpu.VMEM((n_seg, sel, 2 * head), BF16),
            pltpu.VMEM((n_seg, sel, 2 * head), BF16),
            pltpu.VMEM((SEG_DEV, pad, gw), BF16),
            pltpu.VMEM((SEG_DEV, cap, gw), BF16),
            pltpu.VMEM((SEG_DEV, pad, gw), BF16),
            pltpu.VMEM((SEG_DEV, cap, gw), BF16),
            pltpu.VMEM((SEG_DEV, pad, 2 * head), BF16),
            pltpu.VMEM((SEG_DEV, cap, 2 * head), BF16),
            pltpu.VMEM((SEG_DEV, 8, head), F32),
            pltpu.VMEM((n_seg * n_dp, 8, head), F32),
            dma((SEG_DEV,)),
            dma((SEG_DEV,)),
            dma((SEG_DEV,)),
            dma((SEG_DEV,)),
            dma((SEG_DEV,)),
            dma((SEG_DEV,)),
            dma((n_seg,)),
            dma((n_seg,)),
            dma((n_seg,)),
            dma((n_seg,)),
            dma((SEG_DEV,)),
            dma((SEG_DEV,)),
            dma((SEG_DEV,)),
            dma((SEG_DEV,)),
            dma((SEG_DEV,)),
            dma((SEG_DEV,)),
            dma((n_g,)),
            dma((n_g,)),
        ],
        compiler_params=pltpu.CompilerParams(
            collective_id=0, has_side_effects=True, vmem_limit_bytes=56 * 1024 * 1024
        ),
    )(*arguments)
    count = len(results)
    out, gq, gk, gv, gl, gain_q, gain_k = pl.pallas_call(
        place_results,
        out_shape=tuple(jax.ShapeDtypeStruct(r.shape, r.dtype) for r in results),
        in_specs=[anywhere] * count,
        out_specs=(anywhere,) * count,
        scratch_shapes=[pltpu.VMEM(r.shape, r.dtype) for r in results]
        + [dma((count,)), dma((count,))],
        compiler_params=pltpu.CompilerParams(vmem_limit_bytes=56 * 1024 * 1024),
    )(*results)
    return (
        out[None],
        gq[None],
        gk[None],
        gv[None],
        gl,
        gain_q.reshape(head),
        gain_k.reshape(head),
    )


def solution(mesh):
    n_seg = mesh.shape["ctx"] // SEG_DEV
    n_dp = mesh.shape["dp"]
    return jax.shard_map(
        functools.partial(per_device, n_seg, n_dp),
        mesh=mesh,
        in_specs=(
            P("dp", "ctx"),
            P("dp", "ctx", None),
            P("dp", "ctx", None),
            P("dp", "ctx", None),
            P("dp", "ctx"),
            P("dp", "ctx", None),
            P(),
            P(),
        ),
        out_specs=(
            P("dp", "ctx", None),
            P("dp", "ctx", None),
            P("dp", "ctx", None),
            P("dp", "ctx", None),
            P("dp", "ctx"),
            P(),
            P(),
        ),
        check_vma=False,
    )
```
